32 devices in a mesh: grp: 2 (over y), arc: 2 (over x), reg: 4 (over z), sat: 2 (over core).
Axes of the slice: x: 2, y: 2, z: 4, core: 2. Of those that a mesh axis runs over, the one named last changes fastest.
Arguments:
- partials: bfloat16 [64, 8, 2, 128, 256], P(('grp', 'arc', 'reg'), None, 'sat'), parts along dimension 0, may hold values from -0.09375 to 0.09375
- regions: int32 [64, 8], P(('grp', 'arc', 'reg')), parts along dimension 0, may hold values from 0 to 1920, as said below
- observed: float32 [64, 128], P(('grp', 'arc', 'reg')), parts along dimension 0, may hold values from -6 to 6
- weights: float32 [64, 128], P(('grp', 'arc', 'reg')), parts along dimension 0, may hold values from 0.25 to 4
- mascons: float32 [480, 8, 256], P(None, ('grp', 'reg')), parts along dimension 1, may hold values from -6 to 6
- prior: float32 [256], replicated, may hold values from 0.05 to 0.5
Outputs:
- gradient: float32 [480, 8, 256], P(('arc', 'sat'), ('grp', 'reg')), parts along dimension 1
The draws below stay inside these ranges and needn't reach their ends.
There are 2 independent parts, one for each index of `grp`. The reference program is written for one: setup_inputs(seed, part) draws one part's arguments, and reference() takes and returns one part's arrays. A program takes and returns all parts, laid end to end along the dimension named above; an argument that names none is the same for every part. Nothing has to cross between parts.
Inputs may be any that keep to these rules, and one draw needn't show every extreme that they name: Within the 4 arcs of one device along arc+reg (aligned blocks of 4 arcs), at most 8 slots name regions of one owner (region // 480); in every draw some owner gets exactly 8 from every such block. Region 1920 marks an empty slot.
All inputs are finite; a program needn't handle non-finite values.
Results may differ from the reference program's by a relative error of at most 0.0028.
Values may be sent and summed in bfloat16 or wider, within the bound.
No kernel may reach another device: no remote copies, remote signals or barrier semaphores. Data moves between devices by JAX's collectives and lax.ppermute only.
A program may use at most 64 MiB of HBM per device.

```python
import math
import jax
import jax.numpy as jnp
from jax import lax

ARC_DEV = 4
SLOTS = 8
EPOCHS_ARC = 128
MASC = 256
SATS = 2
REG_G = 480
OWNERS = 4
ARC_BLOCKS = 8
ARCS = 32
REGIONS = 1920
CAP = 8


def draw_regions(key, part):
    key = jax.random.fold_in(key, 7)
    key_hot, key_load, key_local, key_order = jax.random.split(key, 4)
    count = ARC_DEV * SLOTS
    hot = jax.random.randint(key_hot, (), 0, OWNERS)
    loads = jax.random.randint(key_load, (ARC_BLOCKS, OWNERS), 0, CAP + 1)
    loads = jnp.where(jnp.arange(OWNERS)[None, :] == hot, CAP, loads)
    ends = jnp.cumsum(loads, axis=1)
    spots = jnp.arange(count)
    owner = jnp.sum((spots[None, :, None] >= ends[:, None, :]).astype(jnp.int32), axis=2)
    local = jax.random.randint(key_local, (ARC_BLOCKS, count), 0, REG_G)
    ids = jnp.where(owner < OWNERS, owner * REG_G + local, REGIONS)
    scores = jax.random.randint(key_order, (ARC_BLOCKS, count), 0, 1 << 20) * count + spots[None, :]
    order = jnp.argsort(scores, axis=1)
    ids = jnp.take_along_axis(ids, order, axis=1)
    return ids.reshape(ARC_BLOCKS * ARC_DEV, SLOTS).astype(jnp.int32)


def levels(key, dims, pieces, smallest, largest):
    factor_of = 1.0
    for dim, blocks in pieces:
        draws = jax.random.uniform(jax.random.fold_in(jax.random.fold_in(key, 6), dim), (blocks,), jnp.float32, smallest / len(pieces), largest / len(pieces))
        factor_of = factor_of * jnp.repeat(jnp.exp(draws), dims[dim] // blocks).reshape((-1,) + (1,) * (len(dims) - 1 - dim))
    return factor_of


def bell_draw(rng, shape, scale, most, cuts=(), held_as=jnp.bfloat16):
    values = jax.random.normal(rng, shape, jnp.float32) * scale
    if len(cuts) > 0:
        values = levels(rng, shape, cuts, -0.22, 0.18) * values
    return jnp.clip(values, min=-most, max=most).astype(held_as)


def setup_inputs(seed: int = 0, part: int = 0) -> dict:
    splits = jax.random.split(jax.random.key(seed), 7)
    part_splits = jax.random.split(jax.random.fold_in(splits[6], part), 7)
    return {
        "partials": bell_draw(part_splits[0], (ARCS, SLOTS, SATS, EPOCHS_ARC, MASC), (SATS * SLOTS * MASC) ** -0.5, 0.09375, ((0, 8), (2, 2))),
        "regions": draw_regions(jax.random.fold_in(jax.random.fold_in(splits[6], part), 71), part),
        "observed": bell_draw(part_splits[2], (ARCS, EPOCHS_ARC), 1.0, 6.0, ((0, 8),), jnp.float32),
        "weights": jnp.clip(jnp.exp(math.log(4.0) - 2.7725887 * jax.random.uniform(part_splits[3], (ARCS, EPOCHS_ARC), jnp.float32) ** levels(part_splits[3], (ARCS, EPOCHS_ARC), ((0, 8),), -0.2, 0.2)), 0.25, 4.0),
        "mascons": bell_draw(part_splits[4], (REG_G, OWNERS, MASC), 1.0, 6.0, ((1, 4),), jnp.float32),
        "prior": jnp.clip(jnp.exp(jax.random.uniform(splits[5], (MASC,), jnp.float32, math.log(0.05), math.log(0.5))), 0.05, 0.5),
    }


def reference(partials, regions, observed, weights, mascons, prior):
    values = mascons.astype(jnp.bfloat16)
    table = jnp.transpose(values, (1, 0, 2)).reshape(REGIONS, MASC)
    table = jnp.concatenate([table, jnp.zeros((1, MASC), jnp.bfloat16)], axis=0)
    rows = table[regions]
    signs = jnp.array([1.0, -1.0], jnp.float32)

    def forward(items):
        block, picked = items
        return jnp.einsum("kstm,km,s->t", block.astype(jnp.float32), picked.astype(jnp.float32), signs)

    predicted = lax.map(forward, (partials, rows))
    weighted = (weights * (observed - predicted)).astype(jnp.bfloat16)

    def backward(items):
        block, resid = items
        return jnp.einsum("kstm,t,s->km", block.astype(jnp.float32), resid.astype(jnp.float32), signs)

    contribution = lax.map(backward, (partials, weighted))
    summed = jax.ops.segment_sum(contribution.reshape(-1, MASC), regions.reshape(-1), num_segments=REGIONS + 1)[:REGIONS]
    summed = jnp.transpose(summed.reshape(OWNERS, REG_G, MASC), (1, 0, 2))
    return summed - prior[None, None, :] * mascons
```

```python
import functools

import jax
import jax.numpy as jnp
from jax import lax
from jax.experimental import pallas as pl
from jax.experimental.pallas import tpu as pltpu
from jax.sharding import PartitionSpec as P

F32, BF16, I32 = jnp.float32, jnp.bfloat16, jnp.int32
VMEM = pltpu.VMEM


def iota(shape, dim):
    return lax.broadcasted_iota(I32, shape, dim)


def transposed_dot(a, b):
    return lax.dot_general(a, b, (((0,), (0,)), ((), ())), preferred_element_type=F32)


def column(refs):
    arcs, slots = refs[0].shape
    rows = [jnp.broadcast_to(ref[a : a + 1, :], (slots, slots)) for ref in refs for a in range(arcs)]
    spread = jnp.concatenate(rows, axis=0)
    mine = iota(spread.shape, 1) == iota(spread.shape, 0) % slots
    return jnp.sum(jnp.where(mine, spread, 0), axis=1, keepdims=True)


def lookup_kernel(cap, *refs):
    n = (len(refs) - 1) // 2
    ids, table, outs = refs[:n], refs[n], refs[n + 1 :]
    group = table.shape[0]
    col = column(ids)
    count = col.shape[0]
    each = count // n
    local = col - lax.axis_index("reg") * group
    owned = (local >= 0) & (local < group)
    onehot = (local == iota((count, group), 1)).astype(F32).astype(BF16)
    dense = jnp.dot(onehot, table[...].astype(BF16), preferred_element_type=F32).astype(BF16)
    row, other = iota((count, count), 0), iota((count, count), 1)
    before = ((other < row) & (other // each == row // each)).astype(F32).astype(BF16)
    members = jnp.broadcast_to(owned.astype(F32), (count, n * cap)).astype(BF16)
    rank = jnp.dot(before, members, preferred_element_type=F32).astype(I32)
    place = rank + (iota(rank.shape, 0) // each) * cap
    pack = (owned & (place == iota(rank.shape, 1))).astype(F32).astype(BF16)
    packed = transposed_dot(pack, dense)
    for k in range(n):
        outs[k][...] = packed[k * cap : (k + 1) * cap].astype(BF16)


def plan_kernel(cap, owners, group, ids, near_ref, far_ref, names_ref):
    me = lax.axis_index("reg")
    col = column([ids])
    count = col.shape[0]
    owner = col // group
    local = col - owner * group
    member = (owner == iota((count, owners), 1)).astype(F32)
    before = (iota((count, count), 1) < iota((count, count), 0)).astype(F32).astype(BF16)
    ahead = jnp.dot(before, member.astype(BF16), preferred_element_type=F32)
    rank = jnp.sum(member * ahead, axis=1, keepdims=True).astype(I32)
    spot = iota((count, owners * cap), 1)
    valid = owner < owners
    near = (valid & (spot == (owner ^ me) * cap + rank)).astype(F32)
    far = (valid & (spot == owner * cap + rank)).astype(F32)
    width = names_ref.shape[1]
    digit = jnp.where(iota((count, width), 1) < width // 2, local // 16, local % 16)
    names = transposed_dot(far.astype(BF16), digit.astype(F32).astype(BF16))
    near_ref[...] = near
    far_ref[...] = far
    names_ref[...] = names


def solve_kernel(cap, copies, *refs):
    n = len(refs) - 7
    rows_in = refs[:n]
    near_ref, far_ref, names_ref, diff, observed, weights, out = refs[n:]
    arcs = observed.shape[1]
    slots = diff.shape[0] // arcs
    came = jnp.concatenate([r[...].astype(F32) for r in rows_in], axis=0).astype(BF16)
    rows = jnp.dot(near_ref[...].astype(BF16), came, preferred_element_type=F32)
    parts = []
    for a in range(arcs):
        total = None
        for k in range(slots):
            i = a * slots + k
            term = diff[i] * rows[i : i + 1, :]
            total = term if total is None else total + term
        predicted = jnp.sum(total, axis=1, keepdims=True)
        weighted = weights[:, a : a + 1] * (observed[:, a : a + 1] - predicted)
        weighted = weighted.astype(BF16).astype(F32)
        for k in range(slots):
            parts.append(jnp.sum(diff[a * slots + k] * weighted, axis=0, keepdims=True))
    contribution = jnp.concatenate(parts, axis=0).astype(BF16)
    packed = transposed_dot(far_ref[...].astype(BF16), contribution)
    for o in range(n):
        both = jnp.concatenate(
            [packed[o * cap : (o + 1) * cap], names_ref[o * cap : (o + 1) * cap]], axis=0
        ).astype(BF16)
        for c in range(copies):
            out[c * n + o] = both


def place_kernel(cap, arrived, current, prior, out):
    sources, _, width = arrived.shape
    share = current.shape[0]
    block = lax.axis_index("arc") * lax.axis_size("sat") + lax.axis_index("sat")
    values, names = [], []
    for s in range(sources):
        got = arrived[s].astype(F32)
        values.append(got[:cap])
        names.append(got[cap:, : width // 2] * 16.0 + got[cap:, width // 2 :])
    values = jnp.concatenate(values, axis=0).astype(BF16)
    local = jnp.concatenate(names, axis=0).astype(I32)
    lanes = local.shape[1] * -(-share // local.shape[1])
    local = jnp.concatenate([local] * (lanes // local.shape[1]), axis=1)
    onehot = (local - block * share == iota(local.shape, 1)).astype(F32).astype(BF16)
    total = transposed_dot(onehot, values)
    out[...] = total[:share] - prior[...] * current[...]


def call(kernel, name, outs, args, flops, size, space=None):
    spec = pl.BlockSpec(memory_space=VMEM)
    return pl.pallas_call(
        kernel,
        out_shape=outs,
        in_specs=[spec] * len(args),
        out_specs=jax.tree.map(lambda _: spec, outs),
        compiler_params=pltpu.CompilerParams(vmem_limit_bytes=16 * 2**20),
        cost_estimate=pl.CostEstimate(flops=flops, bytes_accessed=size, transcendentals=0),
        name=name,
    )(*args)


def per_device(partials, regions, observed, weights, mascons, prior):
    owners, blocks = lax.axis_size("reg"), lax.axis_size("arc")
    arcs, slots = regions.shape
    epochs = observed.shape[1]
    group, width = mascons.shape[0], mascons.shape[2]
    count = arcs * slots
    cap = count // owners
    shape = jax.ShapeDtypeStruct

    def crossing(k):
        return [(r * 2 + s, (r ^ k) * 2 + (1 - s)) for r in range(owners) for s in range(2)]

    asked = [regions] + [lax.ppermute(regions, ("reg", "sat"), crossing(k)) for k in range(1, owners)]
    other = lax.ppermute(partials, "sat", [(0, 1), (1, 0)])
    sign = 1.0 - 2.0 * lax.axis_index("sat").astype(F32)
    diff = sign * (partials.astype(F32) - other.astype(F32))
    diff = diff.reshape(count, epochs, width)
    table = mascons.reshape(group, width)

    found = call(
        functools.partial(lookup_kernel, cap),
        "lookup",
        [shape((cap, width), BF16)] * owners,
        [*asked, table],
        2 * owners * count * group * width,
        group * width * 4,
    )
    came = [found[0]] + [
        lax.ppermute(found[k], ("reg", "sat"), crossing(k)) for k in range(1, owners)
    ]
    near, far, names = call(
        functools.partial(plan_kernel, cap, owners, group),
        "plan",
        [
            shape((count, owners * cap), F32),
            shape((count, owners * cap), F32),
            shape((owners * cap, width), F32),
        ],
        [regions],
        count * count * width,
        count * width * 4,
    )
    sent = call(
        functools.partial(solve_kernel, cap, blocks),
        "solve",
        shape((blocks * owners, 2 * cap, width), BF16),
        [*came, near, far, names, diff, observed.T, weights.T],
        4 * count * epochs * width,
        count * epochs * width * 4,
    )
    arrived = lax.all_to_all(sent, ("arc", "reg"), split_axis=0, concat_axis=0, tiled=True)
    share = group // (blocks * lax.axis_size("sat"))
    block = lax.axis_index("arc") * lax.axis_size("sat") + lax.axis_index("sat")
    current = lax.dynamic_slice_in_dim(table, block * share, share, 0)
    result = call(
        functools.partial(place_kernel, cap),
        "place",
        shape((share, width), F32),
        [arrived, current, prior.reshape(1, width)],
        2 * share * width * blocks * count,
        share * width * 8,
    )
    return result.reshape(share, 1, width)


def solution(mesh):
    placed = (
        P(("grp", "arc", "reg"), None, "sat", None, None),
        P(("grp", "arc", "reg"), None),
        P(("grp", "arc", "reg"), None),
        P(("grp", "arc", "reg"), None),
        P(None, ("grp", "reg"), None),
        P(),
    )
    return jax.shard_map(
        per_device,
        mesh=mesh,
        in_specs=placed,
        out_specs=P(("arc", "sat"), ("grp", "reg"), None),
        check_vma=False,
    )
```

```python
import functools

import jax
import jax.numpy as jnp
from jax import lax
from jax.experimental import pallas as pl
from jax.experimental.pallas import tpu as pltpu
from jax.sharding import PartitionSpec as P

F32, BF16, I32 = jnp.float32, jnp.bfloat16, jnp.int32
VMEM = pltpu.VMEM


def iota(shape, dim):
    return lax.broadcasted_iota(I32, shape, dim)


def transposed_dot(a, b):
    return lax.dot_general(a, b, (((0,), (0,)), ((), ())), preferred_element_type=F32)


def column(refs):
    arcs, slots = refs[0].shape
    rows = [jnp.broadcast_to(ref[a : a + 1, :], (slots, slots)) for ref in refs for a in range(arcs)]
    spread = jnp.concatenate(rows, axis=0)
    mine = iota(spread.shape, 1) == iota(spread.shape, 0) % slots
    return jnp.sum(jnp.where(mine, spread, 0), axis=1, keepdims=True)


def rows_of(local, table):
    onehot = (local == iota((local.shape[0], table.shape[0]), 1)).astype(F32).astype(BF16)
    return jnp.dot(onehot, table[...], preferred_element_type=F32)


def lookup_kernel(cap, *refs):
    n = (len(refs) - 1) // 2
    ids, table, outs = refs[:n], refs[n], refs[n + 1 :]
    group = table.shape[0]
    col = column(ids)
    count = col.shape[0]
    each = count // n
    local = col - lax.axis_index("reg") * group
    owned = (local >= 0) & (local < group)
    dense = rows_of(local, table).astype(BF16)
    row, other = iota((count, count), 0), iota((count, count), 1)
    before = ((other < row) & (other // each == row // each)).astype(F32).astype(BF16)
    members = jnp.broadcast_to(owned.astype(F32), (count, n * cap)).astype(BF16)
    rank = jnp.dot(before, members, preferred_element_type=F32).astype(I32)
    place = rank + (iota(rank.shape, 0) // each) * cap
    pack = (owned & (place == iota(rank.shape, 1))).astype(F32).astype(BF16)
    packed = transposed_dot(pack, dense)
    for k in range(n):
        outs[k][...] = packed[k * cap : (k + 1) * cap].astype(BF16)


def plan_kernel(cap, owners, *refs):
    ins, outs, scratch = refs[:5], refs[5:12], refs[12:]
    table_ref, own_ref, near_ref, far_ref, names_ref, turned_ref, damped_ref = outs
    *held, sems = scratch
    copies = [pltpu.make_async_copy(i, h, sems.at[j]) for j, (i, h) in enumerate(zip(ins, held))]
    for copy in copies:
        copy.start()
    ids, observed, weights, prior, mascons = held
    for copy in copies[:4]:
        copy.wait()
    me = lax.axis_index("reg")
    sign = 1.0 - 2.0 * lax.axis_index("sat").astype(F32)
    group = table_ref.shape[0]
    col = column([ids])
    count = col.shape[0]
    owner = col // group
    local = col - owner * group
    member = (owner == iota((count, owners), 1)).astype(F32)
    before = (iota((count, count), 1) < iota((count, count), 0)).astype(F32).astype(BF16)
    ahead = jnp.dot(before, member.astype(BF16), preferred_element_type=F32)
    rank = jnp.sum(member * ahead, axis=1, keepdims=True).astype(I32)
    valid = owner < owners
    step = owner ^ me
    spot = iota(near_ref.shape, 1)
    near = valid & (step > 0) & (spot == (step - 1) * cap + rank)
    far = (valid & (iota(far_ref.shape, 1) == owner * cap + rank)).astype(F32)
    width = names_ref.shape[1]
    digit = jnp.where(iota((count, width), 1) < width // 2, local // 16, local % 16)
    near_ref[...] = near.astype(F32) * sign
    far_ref[...] = far * sign
    names_ref[...] = transposed_dot(far.astype(BF16), digit.astype(F32).astype(BF16))
    turned_ref[...] = jnp.concatenate([observed[...], weights[...]], axis=0).T
    copies[4].wait()
    table_ref[...] = mascons[:, 0, :].astype(BF16)
    own_ref[...] = rows_of(col - me * group, table_ref) * sign
    share = damped_ref.shape[0]
    block = lax.axis_index("arc") * lax.axis_size("sat") + lax.axis_index("sat")
    damped_ref[...] = prior[...] * mascons[pl.ds(block * share, share), 0, :]


def differ_kernel(own, other, out, held, sems):
    parts = sems.shape[0]
    step = out.shape[0] // parts
    copies = []
    for p in range(parts):
        part = pl.ds(p * step, step)
        copies.append(pltpu.make_async_copy(own.at[part], held.at[part], sems.at[p]))
        copies[-1].start()
    for p in range(parts):
        copies[p].wait()
        for i in range(p * step, (p + 1) * step):
            out[i] = held[i].astype(F32) - other[i].astype(F32)


def solve_kernel(cap, copies, *refs):
    n = len(refs) - 7
    came = refs[:n]
    own_ref, near_ref, far_ref, names_ref, turned, diff, out = refs[n:]
    arcs = turned.shape[1] // 2
    slots = diff.shape[0] // arcs
    came = jnp.concatenate([r[...].astype(F32) for r in came], axis=0).astype(BF16)
    rows = own_ref[...] + jnp.dot(near_ref[...].astype(BF16), came, preferred_element_type=F32)
    parts = []
    for a in range(arcs):
        total = None
        for k in range(slots):
            i = a * slots + k
            term = diff[i] * rows[i : i + 1, :]
            total = term if total is None else total + term
        predicted = jnp.sum(total, axis=1, keepdims=True)
        weighted = turned[:, arcs + a : arcs + a + 1] * (turned[:, a : a + 1] - predicted)
        weighted = weighted.astype(BF16).astype(F32)
        for k in range(slots):
            parts.append(jnp.sum(diff[a * slots + k] * weighted, axis=0, keepdims=True))
    contribution = jnp.concatenate(parts, axis=0).astype(BF16)
    packed = transposed_dot(far_ref[...].astype(BF16), contribution)
    owners = out.shape[0] // copies
    for o in range(owners):
        both = jnp.concatenate(
            [packed[o * cap : (o + 1) * cap], names_ref[o * cap : (o + 1) * cap]], axis=0
        ).astype(BF16)
        for c in range(copies):
            out[c * owners + o] = both


def place_kernel(cap, arrived, damped, out):
    sources, _, width = arrived.shape
    share = out.shape[0]
    block = lax.axis_index("arc") * lax.axis_size("sat") + lax.axis_index("sat")
    values, names = [], []
    for s in range(sources):
        got = arrived[s].astype(F32)
        values.append(got[:cap])
        names.append(got[cap:, : width // 2] * 16.0 + got[cap:, width // 2 :])
    values = jnp.concatenate(values, axis=0).astype(BF16)
    local = jnp.concatenate(names, axis=0).astype(I32)
    local = jnp.concatenate([local] * -(-share // local.shape[1]), axis=1)
    onehot = (local - block * share == iota(local.shape, 1)).astype(F32).astype(BF16)
    total = transposed_dot(onehot, values)
    out[:, 0, :] = total[:share] - damped[...]


def call(kernel, name, outs, args, flops, size, scratch=(), anywhere=()):
    spec, raw = pl.BlockSpec(memory_space=VMEM), pl.BlockSpec(memory_space=pltpu.HBM)
    return pl.pallas_call(
        kernel,
        out_shape=outs,
        in_specs=[raw if i in anywhere else spec for i in range(len(args))],
        out_specs=jax.tree.map(lambda _: spec, outs),
        scratch_shapes=scratch,
        compiler_params=pltpu.CompilerParams(vmem_limit_bytes=16 * 2**20),
        cost_estimate=pl.CostEstimate(flops=flops, bytes_accessed=size, transcendentals=0),
        name=name,
    )(*(pltpu.with_memory_space_constraint(x, pltpu.HBM) if i in anywhere else x for i, x in enumerate(args)))


def per_device(partials, regions, observed, weights, mascons, prior):
    owners, blocks = lax.axis_size("reg"), lax.axis_size("arc")
    arcs, slots = regions.shape
    epochs = observed.shape[1]
    group, width = mascons.shape[0], mascons.shape[2]
    count = arcs * slots
    cap = count // owners
    shape = jax.ShapeDtypeStruct

    def crossing(k):
        return [(r * 2 + s, (r ^ k) * 2 + (1 - s)) for r in range(owners) for s in range(2)]

    names = ("reg", "sat")
    steps = range(1, owners)
    asked = [lax.ppermute(regions, names, crossing(k)) for k in steps]
    other = lax.ppermute(partials, "sat", [(0, 1), (1, 0)])
    share = group // (blocks * lax.axis_size("sat"))
    inputs = [regions, observed, weights, prior.reshape(1, width), mascons]
    table, own, near, far, named, turned, damped = call(
        functools.partial(plan_kernel, cap, owners),
        "plan",
        [
            shape((group, width), BF16),
            shape((count, width), F32),
            shape((count, (owners - 1) * cap), F32),
            shape((count, owners * cap), F32),
            shape((owners * cap, width), F32),
            shape((epochs, 2 * arcs), F32),
            shape((share, width), F32),
        ],
        inputs,
        count * count * width,
        group * width * 4,
        [*(VMEM(i.shape, i.dtype) for i in inputs), pltpu.SemaphoreType.DMA((len(inputs),))],
        range(len(inputs)),
    )
    found = call(
        functools.partial(lookup_kernel, cap),
        "lookup",
        [shape((cap, width), BF16)] * (owners - 1),
        [*asked, table],
        2 * owners * count * group * width,
        group * width * 4,
    )
    came = [lax.ppermute(found[k - 1], names, crossing(k)) for k in steps]
    whole = (count, epochs, width)
    diff = call(
        differ_kernel,
        "differ",
        shape(whole, F32),
        [partials.reshape(whole), other.reshape(whole)],
        count * epochs * width,
        count * epochs * width * 8,
        [VMEM(whole, BF16), pltpu.SemaphoreType.DMA((4,))],
        (0,),
    )
    sent = call(
        functools.partial(solve_kernel, cap, blocks),
        "solve",
        shape((blocks * owners, 2 * cap, width), BF16),
        [*came, own, near, far, named, turned, diff],
        4 * count * epochs * width,
        count * epochs * width * 4,
    )
    arrived = lax.all_to_all(sent, ("arc", "reg"), split_axis=0, concat_axis=0, tiled=True)
    return call(
        functools.partial(place_kernel, cap),
        "place",
        shape((share, 1, width), F32),
        [arrived, damped],
        2 * share * width * blocks * count,
        share * width * 8,
    )


def solution(mesh):
    placed = (
        P(("grp", "arc", "reg"), None, "sat", None, None),
        P(("grp", "arc", "reg"), None),
        P(("grp", "arc", "reg"), None),
        P(("grp", "arc", "reg"), None),
        P(None, ("grp", "reg"), None),
        P(),
    )
    return jax.shard_map(
        per_device,
        mesh=mesh,
        in_specs=placed,
        out_specs=P(("arc", "sat"), ("grp", "reg"), None),
        check_vma=False,
    )
```

```python
import functools

import jax
import jax.numpy as jnp
from jax import lax
from jax.experimental import pallas as pl
from jax.experimental.pallas import tpu as pltpu
from jax.sharding import PartitionSpec as P

F32, BF16, I32 = jnp.float32, jnp.bfloat16, jnp.int32
VMEM = pltpu.VMEM


def iota(shape, dim):
    return lax.broadcasted_iota(I32, shape, dim)


def transposed_dot(a, b):
    return lax.dot_general(a, b, (((0,), (0,)), ((), ())), preferred_element_type=F32)


def column(refs):
    arcs, slots = refs[0].shape
    rows = [jnp.broadcast_to(ref[a : a + 1, :], (slots, slots)) for ref in refs for a in range(arcs)]
    spread = jnp.concatenate(rows, axis=0)
    mine = iota(spread.shape, 1) == iota(spread.shape, 0) % slots
    return jnp.sum(jnp.where(mine, spread, 0), axis=1, keepdims=True)


def rows_of(local, table):
    onehot = (local == iota((local.shape[0], table.shape[0]), 1)).astype(F32).astype(BF16)
    return jnp.dot(onehot, table[...], preferred_element_type=F32)


def lookup_kernel(cap, *refs):
    n = (len(refs) - 1) // 2
    ids, table, outs = refs[:n], refs[n], refs[n + 1 :]
    group = table.shape[0]
    col = column(ids)
    count = col.shape[0]
    each = count // n
    local = col - lax.axis_index("reg") * group
    owned = (local >= 0) & (local < group)
    dense = rows_of(local, table).astype(BF16)
    row, other = iota((count, count), 0), iota((count, count), 1)
    before = ((other < row) & (other // each == row // each)).astype(F32).astype(BF16)
    members = jnp.broadcast_to(owned.astype(F32), (count, n * cap)).astype(BF16)
    rank = jnp.dot(before, members, preferred_element_type=F32).astype(I32)
    place = rank + (iota(rank.shape, 0) // each) * cap
    pack = (owned & (place == iota(rank.shape, 1))).astype(F32).astype(BF16)
    packed = transposed_dot(pack, dense)
    for k in range(n):
        outs[k][...] = packed[k * cap : (k + 1) * cap].astype(BF16)


def plan_kernel(cap, owners, *refs):
    ins, outs, scratch = refs[:5], refs[5:12], refs[12:]
    table_ref, own_ref, near_ref, far_ref, names_ref, turned_ref, damped_ref = outs
    *held, sems = scratch
    copies = [pltpu.make_async_copy(i, h, sems.at[j]) for j, (i, h) in enumerate(zip(ins, held))]
    for copy in copies:
        copy.start()
    ids, observed, weights, prior, mascons = held
    for copy in copies[:4]:
        copy.wait()
    me = lax.axis_index("reg")
    sign = 1.0 - 2.0 * lax.axis_index("sat").astype(F32)
    group = table_ref.shape[0]
    col = column([ids])
    count = col.shape[0]
    owner = col // group
    local = col - owner * group
    member = (owner == iota((count, owners), 1)).astype(F32)
    before = (iota((count, count), 1) < iota((count, count), 0)).astype(F32).astype(BF16)
    ahead = jnp.dot(before, member.astype(BF16), preferred_element_type=F32)
    rank = jnp.sum(member * ahead, axis=1, keepdims=True).astype(I32)
    valid = owner < owners
    step = owner ^ me
    spot = iota(near_ref.shape, 1)
    near = valid & (step > 0) & (spot == (owners - 1 - step) * cap + rank)
    far = (valid & (iota(far_ref.shape, 1) == owner * cap + rank)).astype(F32)
    width = names_ref.shape[1]
    digit = jnp.where(iota((count, width), 1) < width // 2, local // 16, local % 16)
    near_ref[...] = near.astype(F32) * sign
    far_ref[...] = far * sign
    names_ref[...] = transposed_dot(far.astype(BF16), digit.astype(F32).astype(BF16))
    turned_ref[...] = jnp.concatenate([observed[...], weights[...]], axis=0).T
    copies[4].wait()
    table_ref[...] = mascons[:, 0, :].astype(BF16)
    own_ref[...] = rows_of(col - me * group, table_ref) * sign
    share = damped_ref.shape[0]
    block = lax.axis_index("arc") * lax.axis_size("sat") + lax.axis_index("sat")
    damped_ref[...] = prior[...] * mascons[pl.ds(block * share, share), 0, :]


def differ_kernel(own, other, out, held, sems):
    parts = sems.shape[0]
    step = out.shape[0] // parts
    copies = []
    for p in range(parts):
        part = pl.ds(p * step, step)
        copies.append(pltpu.make_async_copy(own.at[part], held.at[part], sems.at[p]))
        copies[-1].start()
    for p in range(parts):
        copies[p].wait()
        for i in range(p * step, (p + 1) * step):
            out[i] = held[i].astype(F32) - other[i].astype(F32)


def solve_kernel(cap, copies, *refs):
    n = len(refs) - 7
    came = refs[:n]
    own_ref, near_ref, far_ref, names_ref, turned, diff, out = refs[n:]
    arcs = turned.shape[1] // 2
    slots = diff.shape[0] // arcs
    came = jnp.concatenate([r[...].astype(F32) for r in came], axis=0).astype(BF16)
    rows = own_ref[...] + jnp.dot(near_ref[...].astype(BF16), came, preferred_element_type=F32)
    parts = []
    for a in range(arcs):
        total = None
        for k in range(slots):
            i = a * slots + k
            term = diff[i] * rows[i : i + 1, :]
            total = term if total is None else total + term
        predicted = jnp.sum(total, axis=1, keepdims=True)
        weighted = turned[:, arcs + a : arcs + a + 1] * (turned[:, a : a + 1] - predicted)
        weighted = weighted.astype(BF16).astype(F32)
        for k in range(slots):
            parts.append(jnp.sum(diff[a * slots + k] * weighted, axis=0, keepdims=True))
    contribution = jnp.concatenate(parts, axis=0).astype(BF16)
    packed = transposed_dot(far_ref[...].astype(BF16), contribution)
    owners = out.shape[0] // copies
    for o in range(owners):
        both = jnp.concatenate(
            [packed[o * cap : (o + 1) * cap], names_ref[o * cap : (o + 1) * cap]], axis=0
        ).astype(BF16)
        for c in range(copies):
            out[c * owners + o] = both


def place_kernel(cap, arrived, damped, out):
    sources, _, width = arrived.shape
    share = out.shape[0]
    block = lax.axis_index("arc") * lax.axis_size("sat") + lax.axis_index("sat")
    values, names = [], []
    for s in range(sources):
        got = arrived[s].astype(F32)
        values.append(got[:cap])
        names.append(got[cap:, : width // 2] * 16.0 + got[cap:, width // 2 :])
    values = jnp.concatenate(values, axis=0).astype(BF16)
    local = jnp.concatenate(names, axis=0).astype(I32)
    local = jnp.concatenate([local] * -(-share // local.shape[1]), axis=1)
    onehot = (local - block * share == iota(local.shape, 1)).astype(F32).astype(BF16)
    total = transposed_dot(onehot, values)
    out[:, 0, :] = total[:share] - damped[...]


def call(kernel, name, outs, args, flops, size, scratch=(), anywhere=()):
    spec, raw = pl.BlockSpec(memory_space=VMEM), pl.BlockSpec(memory_space=pltpu.HBM)
    return pl.pallas_call(
        kernel,
        out_shape=outs,
        in_specs=[raw if i in anywhere else spec for i in range(len(args))],
        out_specs=jax.tree.map(lambda _: spec, outs),
        scratch_shapes=scratch,
        compiler_params=pltpu.CompilerParams(vmem_limit_bytes=16 * 2**20),
        cost_estimate=pl.CostEstimate(flops=flops, bytes_accessed=size, transcendentals=0),
        name=name,
    )(*(pltpu.with_memory_space_constraint(x, pltpu.HBM) if i in anywhere else x for i, x in enumerate(args)))


def per_device(partials, regions, observed, weights, mascons, prior):
    owners, blocks = lax.axis_size("reg"), lax.axis_size("arc")
    arcs, slots = regions.shape
    epochs = observed.shape[1]
    group, width = mascons.shape[0], mascons.shape[2]
    count = arcs * slots
    cap = count // owners
    shape = jax.ShapeDtypeStruct

    def crossing(k):
        return [(r * 2 + s, (r ^ k) * 2 + (1 - s)) for r in range(owners) for s in range(2)]

    names = ("reg", "sat")
    far_first = list(range(owners - 1, 0, -1))
    askers = far_first[1:2] + far_first[:1] + far_first[2:]
    asked = [lax.ppermute(regions, names, crossing(k)) for k in askers]
    other = lax.ppermute(partials, "sat", [(0, 1), (1, 0)])
    share = group // (blocks * lax.axis_size("sat"))
    inputs = [regions, observed, weights, prior.reshape(1, width), mascons]
    table, own, near, far, named, turned, damped = call(
        functools.partial(plan_kernel, cap, owners),
        "plan",
        [
            shape((group, width), BF16),
            shape((count, width), F32),
            shape((count, (owners - 1) * cap), F32),
            shape((count, owners * cap), F32),
            shape((owners * cap, width), F32),
            shape((epochs, 2 * arcs), F32),
            shape((share, width), F32),
        ],
        inputs,
        count * count * width,
        group * width * 4,
        [*(VMEM(i.shape, i.dtype) for i in inputs), pltpu.SemaphoreType.DMA((len(inputs),))],
        range(len(inputs)),
    )
    found = call(
        functools.partial(lookup_kernel, cap),
        "lookup",
        [shape((cap, width), BF16)] * (owners - 1),
        [*asked, table],
        2 * owners * count * group * width,
        group * width * 4,
    )
    came = [lax.ppermute(found[askers.index(k)], names, crossing(k)) for k in far_first]
    whole = (count, epochs, width)
    diff = call(
        differ_kernel,
        "differ",
        shape(whole, F32),
        [partials.reshape(whole), other.reshape(whole)],
        count * epochs * width,
        count * epochs * width * 8,
        [VMEM(whole, BF16), pltpu.SemaphoreType.DMA((4,))],
        (0,),
    )
    sent = call(
        functools.partial(solve_kernel, cap, blocks),
        "solve",
        shape((blocks * owners, 2 * cap, width), BF16),
        [*came, own, near, far, named, turned, diff],
        4 * count * epochs * width,
        count * epochs * width * 4,
    )
    arrived = lax.all_to_all(sent, ("arc", "reg"), split_axis=0, concat_axis=0, tiled=True)
    return call(
        functools.partial(place_kernel, cap),
        "place",
        shape((share, 1, width), F32),
        [arrived, damped],
        2 * share * width * blocks * count,
        share * width * 8,
    )


def solution(mesh):
    placed = (
        P(("grp", "arc", "reg"), None, "sat", None, None),
        P(("grp", "arc", "reg"), None),
        P(("grp", "arc", "reg"), None),
        P(("grp", "arc", "reg"), None),
        P(None, ("grp", "reg"), None),
        P(),
    )
    return jax.shard_map(
        per_device,
        mesh=mesh,
        in_specs=placed,
        out_specs=P(("arc", "sat"), ("grp", "reg"), None),
        check_vma=False,
    )
```

```python
import functools

import jax
import jax.numpy as jnp
from jax import lax
from jax.experimental import pallas as pl
from jax.experimental.pallas import tpu as pltpu
from jax.sharding import PartitionSpec as P

F32, BF16, I32 = jnp.float32, jnp.bfloat16, jnp.int32
VMEM = pltpu.VMEM


def iota(shape, dim):
    return lax.broadcasted_iota(I32, shape, dim)


def transposed_dot(a, b):
    return lax.dot_general(a, b, (((0,), (0,)), ((), ())), preferred_element_type=F32)


def column(refs):
    arcs, slots = refs[0].shape
    rows = [jnp.broadcast_to(ref[a : a + 1, :], (slots, slots)) for ref in refs for a in range(arcs)]
    spread = jnp.concatenate(rows, axis=0)
    mine = iota(spread.shape, 1) == iota(spread.shape, 0) % slots
    return jnp.sum(jnp.where(mine, spread, 0), axis=1, keepdims=True)


def rows_of(local, table):
    onehot = (local == iota((local.shape[0], table.shape[0]), 1)).astype(F32).astype(BF16)
    return jnp.dot(onehot, table[...], preferred_element_type=F32)


def lookup_kernel(cap, *refs):
    n = (len(refs) - 1) // 2
    ids, table, outs = refs[:n], refs[n], refs[n + 1 :]
    group = table.shape[0]
    col = column(ids)
    count = col.shape[0]
    each = count // n
    local = col - lax.axis_index("reg") * group
    owned = (local >= 0) & (local < group)
    dense = rows_of(local, table).astype(BF16)
    row, other = iota((count, count), 0), iota((count, count), 1)
    before = ((other < row) & (other // each == row // each)).astype(F32).astype(BF16)
    members = jnp.broadcast_to(owned.astype(F32), (count, n * cap)).astype(BF16)
    rank = jnp.dot(before, members, preferred_element_type=F32).astype(I32)
    place = rank + (iota(rank.shape, 0) // each) * cap
    pack = (owned & (place == iota(rank.shape, 1))).astype(F32).astype(BF16)
    packed = transposed_dot(pack, dense)
    for k in range(n):
        outs[k][...] = packed[k * cap : (k + 1) * cap].astype(BF16)


def plan_kernel(cap, owners, *refs):
    ins, outs, scratch = refs[:5], refs[5:12], refs[12:]
    table_ref, own_ref, near_ref, far_ref, names_ref, turned_ref, damped_ref = outs
    *held, sems = scratch
    copies = [pltpu.make_async_copy(i, h, sems.at[j]) for j, (i, h) in enumerate(zip(ins, held))]
    for copy in copies:
        copy.start()
    ids, observed, weights, prior, mascons = held
    for copy in copies[:4]:
        copy.wait()
    me = lax.axis_index("reg")
    sign = 1.0 - 2.0 * lax.axis_index("sat").astype(F32)
    group = table_ref.shape[0]
    col = column([ids])
    count = col.shape[0]
    owner = col // group
    local = col - owner * group
    member = (owner == iota((count, owners), 1)).astype(F32)
    before = (iota((count, count), 1) < iota((count, count), 0)).astype(F32).astype(BF16)
    ahead = jnp.dot(before, member.astype(BF16), preferred_element_type=F32)
    rank = jnp.sum(member * ahead, axis=1, keepdims=True).astype(I32)
    valid = owner < owners
    step = owner ^ me
    spot = iota(near_ref.shape, 1)
    near = valid & (step > 0) & (spot == (owners - 1 - step) * cap + rank)
    far = (valid & (iota(far_ref.shape, 1) == step * cap + rank)).astype(F32)
    width = names_ref.shape[1]
    digit = jnp.where(iota((count, width), 1) < width // 2, local // 16, local % 16)
    near_ref[...] = near.astype(F32) * sign
    far_ref[...] = far * sign
    names_ref[...] = transposed_dot(far.astype(BF16), digit.astype(F32).astype(BF16))
    turned_ref[...] = jnp.concatenate([observed[...], weights[...]], axis=0).T
    copies[4].wait()
    table_ref[...] = mascons[:, 0, :].astype(BF16)
    own_ref[...] = rows_of(col - me * group, table_ref) * sign
    share = damped_ref.shape[0]
    block = lax.axis_index("arc") * lax.axis_size("sat") + lax.axis_index("sat")
    damped_ref[...] = prior[...] * mascons[pl.ds(block * share, share), 0, :]


def differ_kernel(own, other, out, held, sems):
    parts = sems.shape[0]
    step = out.shape[0] // parts
    copies = []
    for p in range(parts):
        part = pl.ds(p * step, step)
        copies.append(pltpu.make_async_copy(own.at[part], held.at[part], sems.at[p]))
        copies[-1].start()
    for p in range(parts):
        copies[p].wait()
        for i in range(p * step, (p + 1) * step):
            out[i] = held[i].astype(F32) - other[i].astype(F32)


def solve_kernel(cap, owners, *refs):
    came, outs = refs[: owners - 1], refs[-owners:]
    own_ref, near_ref, far_ref, names_ref, turned, diff = refs[owners - 1 : -owners]
    arcs = turned.shape[1] // 2
    slots = diff.shape[0] // arcs
    came = jnp.concatenate([r[...].astype(F32) for r in came], axis=0).astype(BF16)
    rows = own_ref[...] + jnp.dot(near_ref[...].astype(BF16), came, preferred_element_type=F32)
    parts = []
    for a in range(arcs):
        total = None
        for k in range(slots):
            i = a * slots + k
            term = diff[i] * rows[i : i + 1, :]
            total = term if total is None else total + term
        predicted = jnp.sum(total, axis=1, keepdims=True)
        weighted = turned[:, arcs + a : arcs + a + 1] * (turned[:, a : a + 1] - predicted)
        weighted = weighted.astype(BF16).astype(F32)
        for k in range(slots):
            parts.append(jnp.sum(diff[a * slots + k] * weighted, axis=0, keepdims=True))
    contribution = jnp.concatenate(parts, axis=0).astype(BF16)
    packed = transposed_dot(far_ref[...].astype(BF16), contribution)
    for k in range(owners):
        part = slice(k * cap, (k + 1) * cap)
        outs[k][...] = jnp.concatenate([packed[part], names_ref[part, :]], axis=0).astype(BF16)


def place_kernel(cap, *refs):
    *arrived, damped, out = refs
    share, _, width = out.shape
    block = lax.axis_index("arc") * lax.axis_size("sat") + lax.axis_index("sat")
    values, names = [], []
    for ref in arrived:
        for s in range(ref.shape[0]):
            got = ref[s].astype(F32)
            values.append(got[:cap])
            names.append(got[cap:, : width // 2] * 16.0 + got[cap:, width // 2 :])
    values = jnp.concatenate(values, axis=0).astype(BF16)
    local = jnp.concatenate(names, axis=0).astype(I32)
    local = jnp.concatenate([local] * -(-share // local.shape[1]), axis=1)
    onehot = (local - block * share == iota(local.shape, 1)).astype(F32).astype(BF16)
    total = transposed_dot(onehot, values)
    out[:, 0, :] = total[:share] - damped[...]


def call(kernel, name, outs, args, flops, size, scratch=(), anywhere=()):
    spec, raw = pl.BlockSpec(memory_space=VMEM), pl.BlockSpec(memory_space=pltpu.HBM)
    return pl.pallas_call(
        kernel,
        out_shape=outs,
        in_specs=[raw if i in anywhere else spec for i in range(len(args))],
        out_specs=jax.tree.map(lambda _: spec, outs),
        scratch_shapes=scratch,
        compiler_params=pltpu.CompilerParams(vmem_limit_bytes=16 * 2**20),
        cost_estimate=pl.CostEstimate(flops=flops, bytes_accessed=size, transcendentals=0),
        name=name,
    )(*(pltpu.with_memory_space_constraint(x, pltpu.HBM) if i in anywhere else x for i, x in enumerate(args)))


def per_device(partials, regions, observed, weights, mascons, prior):
    owners, blocks = lax.axis_size("reg"), lax.axis_size("arc")
    arcs, slots = regions.shape
    epochs = observed.shape[1]
    group, width = mascons.shape[0], mascons.shape[2]
    count = arcs * slots
    cap = count // owners
    shape = jax.ShapeDtypeStruct

    def crossing(k):
        return [(r * 2 + s, (r ^ k) * 2 + (1 - s)) for r in range(owners) for s in range(2)]

    names = ("reg", "sat")
    far_first = list(range(owners - 1, 0, -1))
    askers = far_first[1:2] + far_first[:1] + far_first[2:]
    asked = [lax.ppermute(regions, names, crossing(k)) for k in askers]
    other = lax.ppermute(partials, "sat", [(0, 1), (1, 0)])
    share = group // (blocks * lax.axis_size("sat"))
    inputs = [regions, observed, weights, prior.reshape(1, width), mascons]
    table, own, near, far, named, turned, damped = call(
        functools.partial(plan_kernel, cap, owners),
        "plan",
        [
            shape((group, width), BF16),
            shape((count, width), F32),
            shape((count, (owners - 1) * cap), F32),
            shape((count, owners * cap), F32),
            shape((owners * cap, width), F32),
            shape((epochs, 2 * arcs), F32),
            shape((share, width), F32),
        ],
        inputs,
        count * count * width,
        group * width * 4,
        [*(VMEM(i.shape, i.dtype) for i in inputs), pltpu.SemaphoreType.DMA((len(inputs),))],
        range(len(inputs)),
    )
    found = call(
        functools.partial(lookup_kernel, cap),
        "lookup",
        [shape((cap, width), BF16)] * (owners - 1),
        [*asked, table],
        2 * owners * count * group * width,
        group * width * 4,
    )
    came = [lax.ppermute(found[askers.index(k)], names, crossing(k)) for k in far_first]
    whole = (count, epochs, width)
    diff = call(
        differ_kernel,
        "differ",
        shape(whole, F32),
        [partials.reshape(whole), other.reshape(whole)],
        count * epochs * width,
        count * epochs * width * 8,
        [VMEM(whole, BF16), pltpu.SemaphoreType.DMA((4,))],
        (0,),
    )
    sent = call(
        functools.partial(solve_kernel, cap, owners),
        "solve",
        [shape((2 * cap, width), BF16)] * owners,
        [*came, own, near, far, named, turned, diff],
        4 * count * epochs * width,
        count * epochs * width * 4,
    )
    mine = [sent[0]] + [lax.ppermute(sent[k], names, crossing(k)) for k in far_first]
    mine = jnp.stack(mine)
    if blocks == 2:
        over = [(a * 2 + s, (1 - a) * 2 + (1 - s)) for a in range(2) for s in range(2)]
        arrived = [mine, lax.ppermute(mine, ("arc", "sat"), over)]
    else:
        arrived = [lax.all_gather(mine, "arc", tiled=True)]
    return call(
        functools.partial(place_kernel, cap),
        "place",
        shape((share, 1, width), F32),
        [*arrived, damped],
        2 * share * width * blocks * count,
        share * width * 8,
    )


def solution(mesh):
    placed = (
        P(("grp", "arc", "reg"), None, "sat", None, None),
        P(("grp", "arc", "reg"), None),
        P(("grp", "arc", "reg"), None),
        P(("grp", "arc", "reg"), None),
        P(None, ("grp", "reg"), None),
        P(),
    )
    return jax.shard_map(
        per_device,
        mesh=mesh,
        in_specs=placed,
        out_specs=P(("arc", "sat"), ("grp", "reg"), None),
        check_vma=False,
    )
```

```python
import functools

import jax
import jax.numpy as jnp
from jax import lax
from jax.experimental import pallas as pl
from jax.experimental.pallas import tpu as pltpu
from jax.sharding import PartitionSpec as P

F32, BF16, I32 = jnp.float32, jnp.bfloat16, jnp.int32
VMEM = pltpu.VMEM
LANES = 128


def iota(shape, dim):
    return lax.broadcasted_iota(I32, shape, dim)


def transposed_dot(a, b):
    return lax.dot_general(a, b, (((0,), (0,)), ((), ())), preferred_element_type=F32)


def column(refs):
    arcs, slots = refs[0].shape
    rows = [jnp.broadcast_to(ref[a : a + 1, :], (slots, slots)) for ref in refs for a in range(arcs)]
    spread = jnp.concatenate(rows, axis=0)
    mine = iota(spread.shape, 1) == iota(spread.shape, 0) % slots
    return jnp.sum(jnp.where(mine, spread, 0), axis=1, keepdims=True)


def rows_of(local, table):
    onehot = (local == iota((local.shape[0], table.shape[0]), 1)).astype(F32).astype(BF16)
    return jnp.dot(onehot, table[...], preferred_element_type=F32)


def lookup_kernel(cap, *refs):
    n = (len(refs) - 1) // 2
    ids, table, outs = refs[:n], refs[n], refs[n + 1 :]
    group = table.shape[0]
    col = column(ids)
    count = col.shape[0]
    each = count // n
    local = col - lax.axis_index("reg") * group
    owned = (local >= 0) & (local < group)
    dense = rows_of(local, table).astype(BF16)
    row, other = iota((count, count), 0), iota((count, count), 1)
    before = ((other < row) & (other // each == row // each)).astype(F32).astype(BF16)
    members = jnp.broadcast_to(owned.astype(F32), (count, n * cap)).astype(BF16)
    rank = jnp.dot(before, members, preferred_element_type=F32).astype(I32)
    place = rank + (iota(rank.shape, 0) // each) * cap
    pack = (owned & (place == iota(rank.shape, 1))).astype(F32).astype(BF16)
    packed = transposed_dot(pack, dense)
    for k in range(n):
        outs[k][...] = packed[k * cap : (k + 1) * cap].astype(BF16)


def load_kernel(mascons, partials, *refs):
    n = (len(refs) - 4) // 2
    smalls, table, own, outs = refs[:n], refs[n], refs[n + 1], refs[n + 2 : 2 * n + 2]
    held, sems = refs[2 * n + 2 :]
    parts = sems.shape[0] - n - 1
    step = table.shape[0] // parts
    copies = []
    for p in range(parts):
        part = pl.ds(p * step, step)
        copies.append(pltpu.make_async_copy(mascons.at[part], held.at[part], sems.at[p]))
    for j, (i, o) in enumerate(zip((*smalls, partials), (*outs, own))):
        copies.append(pltpu.make_async_copy(i, o, sems.at[parts + j]))
    for copy in copies:
        copy.start()
    for p in range(parts):
        copies[p].wait()
        rows = slice(p * step, (p + 1) * step)
        table[rows, :] = held[rows, 0, :].astype(BF16)
    for copy in copies[parts:]:
        copy.wait()


def plan_kernel(
    cap, owners, ids, observed, weights, table, own_ref, near_ref, far_ref, names_ref, turned_ref
):
    me = lax.axis_index("reg")
    sign = 1.0 - 2.0 * lax.axis_index("sat").astype(F32)
    group = table.shape[0]
    col = column([ids])
    count = col.shape[0]
    own_ref[...] = rows_of(col - me * group, table) * sign
    owner = col // group
    member = (owner == iota((count, owners), 1)).astype(F32)
    before = (iota((count, count), 1) < iota((count, count), 0)).astype(F32).astype(BF16)
    ahead = jnp.dot(before, member.astype(BF16), preferred_element_type=F32)
    rank = jnp.sum(member * ahead, axis=1, keepdims=True).astype(I32)
    valid = owner < owners
    step = owner ^ me
    spot = iota(near_ref.shape, 1)
    near = valid & (step > 0) & (spot == (owners - 1 - step) * cap + rank)
    far = (valid & (iota(far_ref.shape, 1) == step * cap + rank)).astype(F32)
    local = jnp.broadcast_to((col - owner * group - group // 2).astype(F32), (count, names_ref.shape[1]))
    near_ref[...] = near.astype(F32) * sign
    far_ref[...] = far * sign
    names_ref[...] = transposed_dot(far.astype(BF16), local.astype(BF16))
    turned_ref[...] = jnp.concatenate([observed[...], weights[...]], axis=0).T


def differ_kernel(own, other, out):
    for i in range(out.shape[0]):
        out[i] = own[i].astype(F32) - other[i].astype(F32)


def solve_kernel(cap, owners, *refs):
    came, outs = refs[: owners - 1], refs[-owners:]
    own_ref, near_ref, far_ref, names_ref, turned, diff = refs[owners - 1 : -owners]
    arcs = turned.shape[1] // 2
    slots = diff.shape[0] // arcs
    came = jnp.concatenate([r[...].astype(F32) for r in came], axis=0).astype(BF16)
    rows = own_ref[...] + jnp.dot(near_ref[...].astype(BF16), came, preferred_element_type=F32)
    parts = []
    for a in range(arcs):
        total = None
        for k in range(slots):
            i = a * slots + k
            term = diff[i] * rows[i : i + 1, :]
            total = term if total is None else total + term
        predicted = jnp.sum(total, axis=1, keepdims=True)
        weighted = turned[:, arcs + a : arcs + a + 1] * (turned[:, a : a + 1] - predicted)
        weighted = weighted.astype(BF16).astype(F32)
        for k in range(slots):
            parts.append(jnp.sum(diff[a * slots + k] * weighted, axis=0, keepdims=True))
    contribution = jnp.concatenate(parts, axis=0).astype(BF16)
    packed = transposed_dot(far_ref[...].astype(BF16), contribution)
    for k in range(owners):
        part = slice(k * cap, (k + 1) * cap)
        outs[k][...] = jnp.concatenate([packed[part], names_ref[part, :]], axis=1).astype(BF16)


def placed_rows(arrived, group, share, width):
    block = lax.axis_index("arc") * lax.axis_size("sat") + lax.axis_index("sat")
    got = jnp.concatenate([r[s].astype(F32) for r in arrived for s in range(r.shape[0])], axis=0)
    local = got[:, width:].astype(I32) + group // 2 - block * share
    local = jnp.concatenate([local] * -(-share // local.shape[1]), axis=1)
    onehot = (local == iota(local.shape, 1)).astype(F32).astype(BF16)
    return transposed_dot(onehot, got[:, :width].astype(BF16))[:share]


def base_kernel(mascons, prior, *refs):
    *arrived, out, held, sem = refs
    share, width = out.shape
    block = lax.axis_index("arc") * lax.axis_size("sat") + lax.axis_index("sat")
    copy = pltpu.make_async_copy(mascons.at[pl.ds(block * share, share)], held, sem)
    copy.start()
    placed = placed_rows(arrived, mascons.shape[0], share, width) if arrived else 0.0
    copy.wait()
    out[...] = placed - prior[...] * held[:, 0, :]


def place_kernel(group, *refs):
    *arrived, base, out = refs
    share, _, width = out.shape
    out[:, 0, :] = base[...] + placed_rows(arrived, group, share, width)


def call(kernel, name, outs, args, flops, size, scratch=(), anywhere=()):
    spec, raw = pl.BlockSpec(memory_space=VMEM), pl.BlockSpec(memory_space=pltpu.HBM)
    return pl.pallas_call(
        kernel,
        out_shape=outs,
        in_specs=[raw if i in anywhere else spec for i in range(len(args))],
        out_specs=jax.tree.map(lambda _: spec, outs),
        scratch_shapes=scratch,
        compiler_params=pltpu.CompilerParams(vmem_limit_bytes=16 * 2**20),
        cost_estimate=pl.CostEstimate(flops=flops, bytes_accessed=size, transcendentals=0),
        name=name,
    )(*(pltpu.with_memory_space_constraint(x, pltpu.HBM) if i in anywhere else x for i, x in enumerate(args)))


def per_device(partials, regions, observed, weights, mascons, prior):
    owners, blocks = lax.axis_size("reg"), lax.axis_size("arc")
    arcs, slots = regions.shape
    epochs = observed.shape[1]
    group, width = mascons.shape[0], mascons.shape[2]
    count = arcs * slots
    cap = count // owners
    shape = jax.ShapeDtypeStruct

    def crossing(k):
        return [(r * 2 + s, (r ^ k) * 2 + (1 - s)) for r in range(owners) for s in range(2)]

    names = ("reg", "sat")
    share = group // (blocks * lax.axis_size("sat"))
    whole = (count, epochs, width)
    dma = pltpu.SemaphoreType.DMA
    far_first = list(range(owners - 1, 0, -1))
    asked = [lax.ppermute(regions, names, crossing(k)) for k in far_first]
    other = lax.ppermute(partials, "sat", [(0, 1), (1, 0)])
    smalls = [regions, observed, weights]
    table, own_partials, ids, residuals, precisions = call(
        load_kernel,
        "load",
        [shape((group, width), BF16), shape(whole, BF16), *(shape(i.shape, i.dtype) for i in smalls)],
        [mascons, partials.reshape(whole), *smalls],
        group * width,
        group * width * 4,
        [VMEM(mascons.shape, F32), dma((4 + 1 + len(smalls),))],
        range(2 + len(smalls)),
    )
    found = call(
        functools.partial(lookup_kernel, cap),
        "lookup",
        [shape((cap, width), BF16)] * (owners - 1),
        [*asked, table],
        2 * owners * count * group * width,
        group * width * 4,
    )
    came = [lax.ppermute(found[far_first.index(k)], names, crossing(k)) for k in far_first]
    ids, _ = lax.optimization_barrier((ids, found[-1]))
    own, near, far, named, turned = call(
        functools.partial(plan_kernel, cap, owners),
        "plan",
        [
            shape((count, width), F32),
            shape((count, (owners - 1) * cap), F32),
            shape((count, owners * cap), F32),
            shape((owners * cap, LANES), F32),
            shape((epochs, 2 * arcs), F32),
        ],
        [ids, residuals, precisions, table],
        count * count * width,
        count * width * 4,
    )
    diff = call(
        differ_kernel,
        "differ",
        shape(whole, F32),
        [own_partials, other.reshape(whole)],
        count * epochs * width,
        count * epochs * width * 8,
    )
    sent = call(
        functools.partial(solve_kernel, cap, owners),
        "solve",
        [shape((cap, width + LANES), BF16)] * owners,
        [*came, own, near, far, named, turned, diff],
        4 * count * epochs * width,
        count * epochs * width * 4,
    )
    mine = [sent[0]] + [lax.ppermute(sent[k], names, crossing(k)) for k in far_first]
    mine = jnp.stack(mine)
    if blocks == 2:
        over = [(a * 2 + s, (1 - a) * 2 + (1 - s)) for a in range(2) for s in range(2)]
        early, late = [mine], [lax.ppermute(mine, ("arc", "sat"), over)]
    else:
        early, late = [], [lax.all_gather(mine, "arc", tiled=True)]
    base = call(
        base_kernel,
        "base",
        shape((share, width), F32),
        [mascons, prior.reshape(1, width), *early],
        2 * share * width * count,
        share * width * 8,
        [VMEM((share, 1, width), F32), dma],
        (0,),
    )
    return call(
        functools.partial(place_kernel, group),
        "place",
        shape((share, 1, width), F32),
        [*late, base],
        2 * share * width * blocks * count,
        share * width * 8,
    )


def solution(mesh):
    placed = (
        P(("grp", "arc", "reg"), None, "sat", None, None),
        P(("grp", "arc", "reg"), None),
        P(("grp", "arc", "reg"), None),
        P(("grp", "arc", "reg"), None),
        P(None, ("grp", "reg"), None),
        P(),
    )
    return jax.shard_map(
        per_device,
        mesh=mesh,
        in_specs=placed,
        out_specs=P(("arc", "sat"), ("grp", "reg"), None),
        check_vma=False,
    )
```

```python
import functools

import jax
import jax.numpy as jnp
from jax import lax
from jax.experimental import pallas as pl
from jax.experimental.pallas import tpu as pltpu
from jax.sharding import PartitionSpec as P

F32, BF16, I32 = jnp.float32, jnp.bfloat16, jnp.int32
VMEM = pltpu.VMEM
LANES = 128


def iota(shape, dim):
    return lax.broadcasted_iota(I32, shape, dim)


def transposed_dot(a, b):
    return lax.dot_general(a, b, (((0,), (0,)), ((), ())), preferred_element_type=F32)


def column(refs):
    arcs, slots = refs[0].shape
    rows = [jnp.broadcast_to(ref[a : a + 1, :], (slots, slots)) for ref in refs for a in range(arcs)]
    spread = jnp.concatenate(rows, axis=0)
    mine = iota(spread.shape, 1) == iota(spread.shape, 0) % slots
    return jnp.sum(jnp.where(mine, spread, 0), axis=1, keepdims=True)


def rows_of(local, table):
    onehot = (local == iota((local.shape[0], table.shape[0]), 1)).astype(F32).astype(BF16)
    return jnp.dot(onehot, table[...], preferred_element_type=F32)


def lookup_kernel(cap, *refs):
    n = (len(refs) - 1) // 2
    ids, table, outs = refs[:n], refs[n], refs[n + 1 :]
    group = table.shape[0]
    col = column(ids)
    count = col.shape[0]
    each = count // n
    local = col - lax.axis_index("reg") * group
    owned = (local >= 0) & (local < group)
    dense = rows_of(local, table).astype(BF16)
    row, other = iota((count, count), 0), iota((count, count), 1)
    before = ((other < row) & (other // each == row // each)).astype(F32).astype(BF16)
    members = jnp.broadcast_to(owned.astype(F32), (count, n * cap)).astype(BF16)
    rank = jnp.dot(before, members, preferred_element_type=F32).astype(I32)
    place = rank + (iota(rank.shape, 0) // each) * cap
    pack = (owned & (place == iota(rank.shape, 1))).astype(F32).astype(BF16)
    packed = transposed_dot(pack, dense)
    for k in range(n):
        outs[k][...] = packed[k * cap : (k + 1) * cap].astype(BF16)


def load_kernel(mascons, *refs):
    n = (len(refs) - 3) // 2
    smalls, table, outs = refs[:n], refs[n], refs[n + 1 : 2 * n + 1]
    held, sems = refs[2 * n + 1 :]
    parts = sems.shape[0] - n
    step = table.shape[0] // parts
    copies = []
    for p in range(parts):
        part = pl.ds(p * step, step)
        copies.append(pltpu.make_async_copy(mascons.at[part], held.at[part], sems.at[p]))
    for j, (i, o) in enumerate(zip(smalls, outs)):
        copies.append(pltpu.make_async_copy(i, o, sems.at[parts + j]))
    for copy in copies:
        copy.start()
    for p in range(parts):
        copies[p].wait()
        rows = slice(p * step, (p + 1) * step)
        table[rows, :] = held[rows, 0, :].astype(BF16)
    for copy in copies[parts:]:
        copy.wait()


def plan_kernel(cap, owners, order, ids, observed, weights, table, mine, other, *refs):
    own_ref, near_ref, far_ref, names_ref, turned_ref, diff, held, sems = refs
    parts = sems.shape[0]
    size = diff.shape[0] // parts
    copies = []
    for p in range(parts):
        part = pl.ds(p * size, size)
        copies.append(pltpu.make_async_copy(mine.at[part], held.at[part], sems.at[p]))
        copies[-1].start()
    me = lax.axis_index("reg")
    sign = 1.0 - 2.0 * lax.axis_index("sat").astype(F32)
    group = table.shape[0]
    col = column([ids])
    count = col.shape[0]
    own_ref[...] = rows_of(col - me * group, table) * sign
    owner = col // group
    member = (owner == iota((count, owners), 1)).astype(F32)
    before = (iota((count, count), 1) < iota((count, count), 0)).astype(F32).astype(BF16)
    ahead = jnp.dot(before, member.astype(BF16), preferred_element_type=F32)
    rank = jnp.sum(member * ahead, axis=1, keepdims=True).astype(I32)
    valid = owner < owners
    step = owner ^ me
    spot = iota(near_ref.shape, 1)
    turn = sum(jnp.where(step == k, j * cap, 0) for j, k in enumerate(order))
    near = valid & (step > 0) & (spot == turn + rank)
    far = (valid & (iota(far_ref.shape, 1) == step * cap + rank)).astype(F32)
    local = jnp.broadcast_to((col - owner * group - group // 2).astype(F32), (count, names_ref.shape[1]))
    near_ref[...] = near.astype(F32) * sign
    far_ref[...] = far * sign
    names_ref[...] = transposed_dot(far.astype(BF16), local.astype(BF16))
    turned_ref[...] = jnp.concatenate([observed[...], weights[...]], axis=0).T
    for p in range(parts):
        copies[p].wait()
        for i in range(p * size, (p + 1) * size):
            diff[i] = held[i].astype(F32) - other[i].astype(F32)


def solve_kernel(cap, owners, *refs):
    came, outs = refs[: owners - 1], refs[-owners:]
    own_ref, near_ref, far_ref, names_ref, turned, diff = refs[owners - 1 : -owners]
    arcs = turned.shape[1] // 2
    slots = diff.shape[0] // arcs
    came = jnp.concatenate([r[...].astype(F32) for r in came], axis=0).astype(BF16)
    rows = own_ref[...] + jnp.dot(near_ref[...].astype(BF16), came, preferred_element_type=F32)
    parts = []
    for a in range(arcs):
        total = None
        for k in range(slots):
            i = a * slots + k
            term = diff[i] * rows[i : i + 1, :]
            total = term if total is None else total + term
        predicted = jnp.sum(total, axis=1, keepdims=True)
        weighted = turned[:, arcs + a : arcs + a + 1] * (turned[:, a : a + 1] - predicted)
        weighted = weighted.astype(BF16).astype(F32)
        for k in range(slots):
            parts.append(jnp.sum(diff[a * slots + k] * weighted, axis=0, keepdims=True))
    contribution = jnp.concatenate(parts, axis=0).astype(BF16)
    packed = transposed_dot(far_ref[...].astype(BF16), contribution)
    for k in range(owners):
        part = slice(k * cap, (k + 1) * cap)
        outs[k][...] = jnp.concatenate([packed[part], names_ref[part, :]], axis=1).astype(BF16)


def placed_rows(arrived, group, share, width):
    block = lax.axis_index("arc") * lax.axis_size("sat") + lax.axis_index("sat")
    got = jnp.concatenate([r[s].astype(F32) for r in arrived for s in range(r.shape[0])], axis=0)
    local = got[:, width:].astype(I32) + group // 2 - block * share
    local = jnp.concatenate([local] * -(-share // local.shape[1]), axis=1)
    onehot = (local == iota(local.shape, 1)).astype(F32).astype(BF16)
    return transposed_dot(onehot, got[:, :width].astype(BF16))[:share]


def base_kernel(mascons, prior, *refs):
    *arrived, out, held, sem = refs
    share, width = out.shape
    block = lax.axis_index("arc") * lax.axis_size("sat") + lax.axis_index("sat")
    copy = pltpu.make_async_copy(mascons.at[pl.ds(block * share, share)], held, sem)
    copy.start()
    placed = placed_rows(arrived, mascons.shape[0], share, width) if arrived else 0.0
    copy.wait()
    out[...] = placed - prior[...] * held[:, 0, :]


def place_kernel(group, *refs):
    *arrived, base, out = refs
    share, _, width = out.shape
    out[:, 0, :] = base[...] + placed_rows(arrived, group, share, width)


def call(kernel, name, outs, args, flops, size, scratch=(), anywhere=()):
    spec, raw = pl.BlockSpec(memory_space=VMEM), pl.BlockSpec(memory_space=pltpu.HBM)
    return pl.pallas_call(
        kernel,
        out_shape=outs,
        in_specs=[raw if i in anywhere else spec for i in range(len(args))],
        out_specs=jax.tree.map(lambda _: spec, outs),
        scratch_shapes=scratch,
        compiler_params=pltpu.CompilerParams(vmem_limit_bytes=16 * 2**20),
        cost_estimate=pl.CostEstimate(flops=flops, bytes_accessed=size, transcendentals=0),
        name=name,
    )(*(pltpu.with_memory_space_constraint(x, pltpu.HBM) if i in anywhere else x for i, x in enumerate(args)))


def per_device(partials, regions, observed, weights, mascons, prior):
    owners, blocks = lax.axis_size("reg"), lax.axis_size("arc")
    arcs, slots = regions.shape
    epochs = observed.shape[1]
    group, width = mascons.shape[0], mascons.shape[2]
    count = arcs * slots
    cap = count // owners
    shape = jax.ShapeDtypeStruct

    def crossing(k):
        return [(r * 2 + s, (r ^ k) * 2 + (1 - s)) for r in range(owners) for s in range(2)]

    names = ("reg", "sat")
    share = group // (blocks * lax.axis_size("sat"))
    whole = (count, epochs, width)
    dma = pltpu.SemaphoreType.DMA
    far_first = list(range(owners - 1, 0, -1))
    order = far_first[::-1]
    asked = {k: lax.ppermute(regions, names, crossing(k)) for k in far_first}
    other = lax.ppermute(partials, "sat", [(0, 1), (1, 0)])
    smalls = [regions, observed, weights]
    table, ids, residuals, precisions = call(
        load_kernel,
        "load",
        [shape((group, width), BF16), *(shape(i.shape, i.dtype) for i in smalls)],
        [mascons, *smalls],
        group * width,
        group * width * 4,
        [VMEM(mascons.shape, F32), dma((4 + len(smalls),))],
        range(1 + len(smalls)),
    )
    found = {}
    for some in filter(None, (far_first[1:2], far_first[:1] + far_first[2:])):
        found |= zip(
            some,
            call(
                functools.partial(lookup_kernel, cap),
                "lookup",
                [shape((cap, width), BF16)] * len(some),
                [*(asked[k] for k in some), table],
                2 * len(some) * count * group * width,
                group * width * 4,
            ),
        )
    came = [lax.ppermute(found[k], names, crossing(k)) for k in order]
    ids, _ = lax.optimization_barrier((ids, found[order[0]]))
    own, near, far, named, turned, diff = call(
        functools.partial(plan_kernel, cap, owners, order),
        "plan",
        [
            shape((count, width), F32),
            shape((count, (owners - 1) * cap), F32),
            shape((count, owners * cap), F32),
            shape((owners * cap, LANES), F32),
            shape((epochs, 2 * arcs), F32),
            shape(whole, F32),
        ],
        [ids, residuals, precisions, table, partials.reshape(whole), other.reshape(whole)],
        count * epochs * width,
        count * epochs * width * 8,
        [VMEM(whole, BF16), dma((4,))],
        (4,),
    )
    sent = call(
        functools.partial(solve_kernel, cap, owners),
        "solve",
        [shape((cap, width + LANES), BF16)] * owners,
        [*came, own, near, far, named, turned, diff],
        4 * count * epochs * width,
        count * epochs * width * 4,
    )
    mine = [sent[0]] + [lax.ppermute(sent[k], names, crossing(k)) for k in far_first]
    mine = jnp.stack(mine)
    if blocks == 2:
        over = [(a * 2 + s, (1 - a) * 2 + (1 - s)) for a in range(2) for s in range(2)]
        early, late = [mine], [lax.ppermute(mine, ("arc", "sat"), over)]
    else:
        early, late = [], [lax.all_gather(mine, "arc", tiled=True)]
    base = call(
        base_kernel,
        "base",
        shape((share, width), F32),
        [mascons, prior.reshape(1, width), *early],
        2 * share * width * count,
        share * width * 8,
        [VMEM((share, 1, width), F32), dma],
        (0,),
    )
    return call(
        functools.partial(place_kernel, group),
        "place",
        shape((share, 1, width), F32),
        [*late, base],
        2 * share * width * blocks * count,
        share * width * 8,
    )


def solution(mesh):
    placed = (
        P(("grp", "arc", "reg"), None, "sat", None, None),
        P(("grp", "arc", "reg"), None),
        P(("grp", "arc", "reg"), None),
        P(("grp", "arc", "reg"), None),
        P(None, ("grp", "reg"), None),
        P(),
    )
    return jax.shard_map(
        per_device,
        mesh=mesh,
        in_specs=placed,
        out_specs=P(("arc", "sat"), ("grp", "reg"), None),
        check_vma=False,
    )
```

```python
import functools

import jax
import jax.numpy as jnp
from jax import lax
from jax.experimental import pallas as pl
from jax.experimental.pallas import tpu as pltpu
from jax.sharding import PartitionSpec as P

F32, BF16, I32 = jnp.float32, jnp.bfloat16, jnp.int32
VMEM = pltpu.VMEM
LANES = 128


def iota(shape, dim):
    return lax.broadcasted_iota(I32, shape, dim)


def transposed_dot(a, b):
    return lax.dot_general(a, b, (((0,), (0,)), ((), ())), preferred_element_type=F32)


def column(refs):
    arcs, slots = refs[0].shape
    rows = [jnp.broadcast_to(ref[a : a + 1, :], (slots, slots)) for ref in refs for a in range(arcs)]
    spread = jnp.concatenate(rows, axis=0)
    mine = iota(spread.shape, 1) == iota(spread.shape, 0) % slots
    return jnp.sum(jnp.where(mine, spread, 0), axis=1, keepdims=True)


def rows_of(local, table):
    onehot = (local == iota((local.shape[0], table.shape[0]), 1)).astype(F32).astype(BF16)
    return jnp.dot(onehot, table[...], preferred_element_type=F32)


def lookup_kernel(cap, *refs):
    n = (len(refs) - 1) // 2
    ids, table, outs = refs[:n], refs[n], refs[n + 1 :]
    group = table.shape[0]
    col = column(ids)
    count = col.shape[0]
    each = count // n
    local = col - lax.axis_index("reg") * group
    owned = (local >= 0) & (local < group)
    dense = rows_of(local, table).astype(BF16)
    row, other = iota((count, count), 0), iota((count, count), 1)
    before = ((other < row) & (other // each == row // each)).astype(F32).astype(BF16)
    members = jnp.broadcast_to(owned.astype(F32), (count, n * cap)).astype(BF16)
    rank = jnp.dot(before, members, preferred_element_type=F32).astype(I32)
    place = rank + (iota(rank.shape, 0) // each) * cap
    pack = (owned & (place == iota(rank.shape, 1))).astype(F32).astype(BF16)
    packed = transposed_dot(pack, dense)
    for k in range(n):
        outs[k][...] = packed[k * cap : (k + 1) * cap].astype(BF16)


def load_kernel(mascons, *refs):
    n = (len(refs) - 3) // 2
    smalls, table, outs = refs[:n], refs[n], refs[n + 1 : 2 * n + 1]
    held, sems = refs[2 * n + 1 :]
    parts = sems.shape[0] - n
    step = table.shape[0] // parts
    copies = []
    for p in range(parts):
        part = pl.ds(p * step, step)
        copies.append(pltpu.make_async_copy(mascons.at[part, 0, :], held.at[part], sems.at[p]))
    for j, (i, o) in enumerate(zip(smalls, outs)):
        copies.append(pltpu.make_async_copy(i, o, sems.at[parts + j]))
    for copy in copies:
        copy.start()
    for p in range(parts):
        copies[p].wait()
        rows = slice(p * step, (p + 1) * step)
        table[rows, :] = held[rows, :].astype(BF16)
    for copy in copies[parts:]:
        copy.wait()


def plan_kernel(cap, owners, pairs, ids, observed, weights, table, mine, other, *refs):
    own_ref, near_ref, far_ref, names_ref, turned_ref, diff, held, sems = refs
    parts = sems.shape[0]
    size = diff.shape[0] // parts
    copies = []
    for p in range(parts):
        part = pl.ds(p * size, size)
        copies.append(pltpu.make_async_copy(mine.at[part], held.at[part], sems.at[p]))
        copies[-1].start()
    me = lax.axis_index("reg")
    sign = 1.0 - 2.0 * lax.axis_index("sat").astype(F32)
    group = table.shape[0]
    col = column([ids])
    count = col.shape[0]
    own_ref[...] = rows_of(col - me * group, table) * sign
    owner = col // group
    member = (owner == iota((count, owners), 1)).astype(F32)
    before = (iota((count, count), 1) < iota((count, count), 0)).astype(F32).astype(BF16)
    ahead = jnp.dot(before, member.astype(BF16), preferred_element_type=F32)
    rank = jnp.sum(member * ahead, axis=1, keepdims=True).astype(I32)
    valid = owner < owners
    step = owner ^ me
    spot = iota(near_ref.shape, 1)
    sat = lax.axis_index("sat")
    turn = jnp.where(step == 1, 2 * len(pairs) * cap, 0)
    for j, (high, low) in enumerate(pairs):
        turn += jnp.where(step == high, (2 * j + sat) * cap, 0)
        turn += jnp.where(step == low, (2 * j + 1 - sat) * cap, 0)
    near = valid & (step > 0) & (spot == turn + rank)
    far = (valid & (iota(far_ref.shape, 1) == step * cap + rank)).astype(F32)
    local = jnp.broadcast_to((col - owner * group - group // 2).astype(F32), (count, names_ref.shape[1]))
    near_ref[...] = near.astype(F32) * sign
    far_ref[...] = far * sign
    names_ref[...] = transposed_dot(far.astype(BF16), local.astype(BF16))
    turned_ref[...] = jnp.concatenate([observed[...], weights[...]], axis=0).T
    for p in range(parts):
        copies[p].wait()
        for i in range(p * size, (p + 1) * size):
            diff[i] = held[i].astype(F32) - other[i].astype(F32)


def solve_kernel(cap, owners, *refs):
    came, outs = refs[: owners - 1], refs[-owners:]
    own_ref, near_ref, far_ref, names_ref, turned, diff = refs[owners - 1 : -owners]
    arcs = turned.shape[1] // 2
    slots = diff.shape[0] // arcs
    came = jnp.concatenate([r[...].astype(F32) for r in came], axis=0).astype(BF16)
    rows = own_ref[...] + jnp.dot(near_ref[...].astype(BF16), came, preferred_element_type=F32)
    parts = []
    for a in range(arcs):
        total = None
        for k in range(slots):
            i = a * slots + k
            term = diff[i] * rows[i : i + 1, :]
            total = term if total is None else total + term
        predicted = jnp.sum(total, axis=1, keepdims=True)
        weighted = turned[:, arcs + a : arcs + a + 1] * (turned[:, a : a + 1] - predicted)
        weighted = weighted.astype(BF16).astype(F32)
        for k in range(slots):
            parts.append(jnp.sum(diff[a * slots + k] * weighted, axis=0, keepdims=True))
    contribution = jnp.concatenate(parts, axis=0).astype(BF16)
    packed = transposed_dot(far_ref[...].astype(BF16), contribution)
    for k in range(owners):
        part = slice(k * cap, (k + 1) * cap)
        outs[k][...] = jnp.concatenate([packed[part], names_ref[part, :]], axis=1).astype(BF16)


def placed_rows(arrived, group, share, width):
    block = lax.axis_index("arc") * lax.axis_size("sat") + lax.axis_index("sat")
    got = jnp.concatenate([r[s].astype(F32) for r in arrived for s in range(r.shape[0])], axis=0)
    local = got[:, width:].astype(I32) + group // 2 - block * share
    local = jnp.concatenate([local] * -(-share // local.shape[1]), axis=1)
    onehot = (local == iota(local.shape, 1)).astype(F32).astype(BF16)
    return transposed_dot(onehot, got[:, :width].astype(BF16))[:share]


def base_kernel(mascons, prior, *refs):
    *arrived, out, held, sem = refs
    share, width = out.shape
    block = lax.axis_index("arc") * lax.axis_size("sat") + lax.axis_index("sat")
    copy = pltpu.make_async_copy(mascons.at[pl.ds(block * share, share)], held, sem)
    copy.start()
    placed = placed_rows(arrived, mascons.shape[0], share, width) if arrived else 0.0
    copy.wait()
    out[...] = placed - prior[...] * held[:, 0, :]


def place_kernel(group, *refs):
    *arrived, base, out = refs
    share, _, width = out.shape
    out[:, 0, :] = base[...] + placed_rows(arrived, group, share, width)


def call(kernel, name, outs, args, flops, size, scratch=(), anywhere=()):
    spec, raw = pl.BlockSpec(memory_space=VMEM), pl.BlockSpec(memory_space=pltpu.HBM)
    return pl.pallas_call(
        kernel,
        out_shape=outs,
        in_specs=[raw if i in anywhere else spec for i in range(len(args))],
        out_specs=jax.tree.map(lambda _: spec, outs),
        scratch_shapes=scratch,
        compiler_params=pltpu.CompilerParams(vmem_limit_bytes=16 * 2**20),
        cost_estimate=pl.CostEstimate(flops=flops, bytes_accessed=size, transcendentals=0),
        name=name,
    )(*(pltpu.with_memory_space_constraint(x, pltpu.HBM) if i in anywhere else x for i, x in enumerate(args)))


def per_device(partials, regions, observed, weights, mascons, prior):
    owners, blocks = lax.axis_size("reg"), lax.axis_size("arc")
    arcs, slots = regions.shape
    epochs = observed.shape[1]
    group, width = mascons.shape[0], mascons.shape[2]
    count = arcs * slots
    cap = count // owners
    shape = jax.ShapeDtypeStruct

    def crossing(even, odd):
        return [
            (r * 2 + s, (r ^ (odd if s else even)) * 2 + (1 - s)) for r in range(owners) for s in range(2)
        ]

    names = ("reg", "sat")
    share = group // (blocks * lax.axis_size("sat"))
    whole = (count, epochs, width)
    dma = pltpu.SemaphoreType.DMA
    far_first = list(range(owners - 1, 0, -1))
    pairs = [(k + 1, k) for k in range(owners - 2, 0, -2)]
    hands = [(1, 1), *pairs]
    asked = {h: lax.ppermute(regions, names, crossing(*h)) for h in hands}
    other = lax.ppermute(partials, "sat", [(0, 1), (1, 0)])
    smalls = [regions, observed, weights]
    table, ids, residuals, precisions = call(
        load_kernel,
        "load",
        [shape((group, width), BF16), *(shape(i.shape, i.dtype) for i in smalls)],
        [mascons, *smalls],
        group * width,
        group * width * 4,
        [VMEM((group, width), F32), dma((4 + len(smalls),))],
        range(1 + len(smalls)),
    )
    found = call(
        functools.partial(lookup_kernel, cap),
        "lookup",
        [shape((cap, width), BF16)] * len(hands),
        [*(asked[h] for h in hands), table],
        2 * len(hands) * count * group * width,
        group * width * 4,
    )
    found = dict(zip(hands, found))
    came = {h: lax.ppermute(found[h], names, crossing(*h[::-1])) for h in hands}
    ids, _ = lax.optimization_barrier((ids, found[(1, 1)]))
    own, near, far, named, turned, diff = call(
        functools.partial(plan_kernel, cap, owners, pairs),
        "plan",
        [
            shape((count, width), F32),
            shape((count, (owners - 1) * cap), F32),
            shape((count, owners * cap), F32),
            shape((owners * cap, LANES), F32),
            shape((epochs, 2 * arcs), F32),
            shape(whole, F32),
        ],
        [ids, residuals, precisions, table, partials.reshape(whole), other.reshape(whole)],
        count * epochs * width,
        count * epochs * width * 8,
        [VMEM(whole, BF16), dma((4,))],
        (4,),
    )
    arrived = []
    for h in pairs:
        rows, _ = lax.optimization_barrier((came[h], turned))
        arrived += [came[h], lax.ppermute(rows, "sat", [(0, 1), (1, 0)])]
    arrived.append(came[1, 1])
    sent = call(
        functools.partial(solve_kernel, cap, owners),
        "solve",
        [shape((cap, width + LANES), BF16)] * owners,
        [*arrived, own, near, far, named, turned, diff],
        4 * count * epochs * width,
        count * epochs * width * 4,
    )
    mine = [sent[0]] + [lax.ppermute(sent[k], names, crossing(k, k)) for k in far_first]
    mine = jnp.stack(mine)
    if blocks == 2:
        over = [(a * 2 + s, (1 - a) * 2 + (1 - s)) for a in range(2) for s in range(2)]
        early, late = [mine], [lax.ppermute(mine, ("arc", "sat"), over)]
    else:
        early, late = [], [lax.all_gather(mine, "arc", tiled=True)]
    base = call(
        base_kernel,
        "base",
        shape((share, width), F32),
        [mascons, prior.reshape(1, width), *early],
        2 * share * width * count,
        share * width * 8,
        [VMEM((share, 1, width), F32), dma],
        (0,),
    )
    return call(
        functools.partial(place_kernel, group),
        "place",
        shape((share, 1, width), F32),
        [*late, base],
        2 * share * width * blocks * count,
        share * width * 8,
    )


def solution(mesh):
    placed = (
        P(("grp", "arc", "reg"), None, "sat", None, None),
        P(("grp", "arc", "reg"), None),
        P(("grp", "arc", "reg"), None),
        P(("grp", "arc", "reg"), None),
        P(None, ("grp", "reg"), None),
        P(),
    )
    return jax.shard_map(
        per_device,
        mesh=mesh,
        in_specs=placed,
        out_specs=P(("arc", "sat"), ("grp", "reg"), None),
        check_vma=False,
    )
```

```python
import functools

import jax
import jax.numpy as jnp
from jax import lax
from jax.experimental import pallas as pl
from jax.experimental.pallas import tpu as pltpu
from jax.sharding import PartitionSpec as P

F32, BF16, I32 = jnp.float32, jnp.bfloat16, jnp.int32
VMEM = pltpu.VMEM
LANES = 128


def iota(shape, dim):
    return lax.broadcasted_iota(I32, shape, dim)


def transposed_dot(a, b):
    return lax.dot_general(a, b, (((0,), (0,)), ((), ())), preferred_element_type=F32)


def column(refs):
    arcs, slots = refs[0].shape
    rows = [jnp.broadcast_to(ref[a : a + 1, :], (slots, slots)) for ref in refs for a in range(arcs)]
    spread = jnp.concatenate(rows, axis=0)
    mine = iota(spread.shape, 1) == iota(spread.shape, 0) % slots
    return jnp.sum(jnp.where(mine, spread, 0), axis=1, keepdims=True)


def rows_of(local, table):
    onehot = (local == iota((local.shape[0], table.shape[0]), 1)).astype(F32).astype(BF16)
    return jnp.dot(onehot, table[...], preferred_element_type=F32)


def lookup_kernel(cap, *refs):
    n = (len(refs) - 1) // 2
    ids, table, outs = refs[:n], refs[n], refs[n + 1 :]
    group = table.shape[0]
    col = column(ids)
    count = col.shape[0]
    each = count // n
    local = col - lax.axis_index("reg") * group
    owned = (local >= 0) & (local < group)
    dense = rows_of(local, table).astype(BF16)
    row, other = iota((count, count), 0), iota((count, count), 1)
    before = ((other < row) & (other // each == row // each)).astype(F32).astype(BF16)
    members = jnp.broadcast_to(owned.astype(F32), (count, n * cap)).astype(BF16)
    rank = jnp.dot(before, members, preferred_element_type=F32).astype(I32)
    place = rank + (iota(rank.shape, 0) // each) * cap
    pack = (owned & (place == iota(rank.shape, 1))).astype(F32).astype(BF16)
    packed = transposed_dot(pack, dense)
    for k in range(n):
        outs[k][...] = packed[k * cap : (k + 1) * cap].astype(BF16)


def load_kernel(mascons, *refs):
    n = (len(refs) - 3) // 2
    others, table, outs = refs[:n], refs[n], refs[n + 1 : 2 * n + 1]
    held, sems = refs[2 * n + 1 :]
    parts = sems.shape[0] - n
    step = table.shape[0] // parts
    copies = []
    for p in range(parts):
        part = pl.ds(p * step, step)
        copies.append(pltpu.make_async_copy(mascons.at[part, 0, :], held.at[part], sems.at[p]))
    for j, (i, o) in enumerate(zip(others, outs)):
        copies.append(pltpu.make_async_copy(i, o, sems.at[parts + j]))
    for copy in copies:
        copy.start()
    for p in range(parts):
        copies[p].wait()
        rows = slice(p * step, (p + 1) * step)
        table[rows, :] = held[rows, :].astype(BF16)
    for copy in copies[parts:]:
        copy.wait()


def plan_kernel(cap, owners, pairs, ids, observed, weights, table, *refs):
    own_ref, near_ref, far_ref, names_ref, turned_ref = refs
    me = lax.axis_index("reg")
    sign = 1.0 - 2.0 * lax.axis_index("sat").astype(F32)
    group = table.shape[0]
    col = column([ids])
    count = col.shape[0]
    own_ref[...] = rows_of(col - me * group, table) * sign
    owner = col // group
    member = (owner == iota((count, owners), 1)).astype(F32)
    before = (iota((count, count), 1) < iota((count, count), 0)).astype(F32).astype(BF16)
    ahead = jnp.dot(before, member.astype(BF16), preferred_element_type=F32)
    rank = jnp.sum(member * ahead, axis=1, keepdims=True).astype(I32)
    valid = owner < owners
    step = owner ^ me
    spot = iota(near_ref.shape, 1)
    sat = lax.axis_index("sat")
    turn = jnp.where(step == 1, 2 * len(pairs) * cap, 0)
    for j, (high, low) in enumerate(pairs):
        turn += jnp.where(step == high, (2 * j + sat) * cap, 0)
        turn += jnp.where(step == low, (2 * j + 1 - sat) * cap, 0)
    near = valid & (step > 0) & (spot == turn + rank)
    far = (valid & (iota(far_ref.shape, 1) == step * cap + rank)).astype(F32)
    local = jnp.broadcast_to((col - owner * group - group // 2).astype(F32), (count, names_ref.shape[1]))
    near_ref[...] = near.astype(F32) * sign
    far_ref[...] = far * sign
    names_ref[...] = transposed_dot(far.astype(BF16), local.astype(BF16))
    turned_ref[...] = jnp.concatenate([observed[...], weights[...]], axis=0).T


def differ_kernel(mine, other, diff):
    for i in range(diff.shape[0]):
        diff[i] = mine[i].astype(F32) - other[i].astype(F32)


def solve_kernel(cap, owners, *refs):
    came, outs = refs[: owners - 1], refs[-owners:]
    own_ref, near_ref, far_ref, names_ref, turned, diff = refs[owners - 1 : -owners]
    arcs = turned.shape[1] // 2
    slots = diff.shape[0] // arcs
    came = jnp.concatenate([r[...].astype(F32) for r in came], axis=0).astype(BF16)
    rows = own_ref[...] + jnp.dot(near_ref[...].astype(BF16), came, preferred_element_type=F32)
    parts = []
    for a in range(arcs):
        total = None
        for k in range(slots):
            i = a * slots + k
            term = diff[i] * rows[i : i + 1, :]
            total = term if total is None else total + term
        predicted = jnp.sum(total, axis=1, keepdims=True)
        weighted = turned[:, arcs + a : arcs + a + 1] * (turned[:, a : a + 1] - predicted)
        weighted = weighted.astype(BF16).astype(F32)
        for k in range(slots):
            parts.append(jnp.sum(diff[a * slots + k] * weighted, axis=0, keepdims=True))
    contribution = jnp.concatenate(parts, axis=0).astype(BF16)
    packed = transposed_dot(far_ref[...].astype(BF16), contribution)
    for k in range(owners):
        part = slice(k * cap, (k + 1) * cap)
        outs[k][...] = jnp.concatenate([packed[part], names_ref[part, :]], axis=1).astype(BF16)


def placed_rows(arrived, group, share, width):
    block = lax.axis_index("arc") * lax.axis_size("sat") + lax.axis_index("sat")
    got = jnp.concatenate([r[s].astype(F32) for r in arrived for s in range(r.shape[0])], axis=0)
    local = got[:, width:].astype(I32) + group // 2 - block * share
    local = jnp.concatenate([local] * -(-share // local.shape[1]), axis=1)
    onehot = (local == iota(local.shape, 1)).astype(F32).astype(BF16)
    return transposed_dot(onehot, got[:, :width].astype(BF16))[:share]


def base_kernel(mascons, prior, *refs):
    *arrived, out, held, sem = refs
    share, width = out.shape
    block = lax.axis_index("arc") * lax.axis_size("sat") + lax.axis_index("sat")
    copy = pltpu.make_async_copy(mascons.at[pl.ds(block * share, share)], held, sem)
    copy.start()
    placed = placed_rows(arrived, mascons.shape[0], share, width) if arrived else 0.0
    copy.wait()
    out[...] = placed - prior[...] * held[:, 0, :]


def place_kernel(group, *refs):
    *arrived, base, out = refs
    share, _, width = out.shape
    out[:, 0, :] = base[...] + placed_rows(arrived, group, share, width)


def call(kernel, name, outs, args, flops, size, scratch=(), anywhere=()):
    spec, raw = pl.BlockSpec(memory_space=VMEM), pl.BlockSpec(memory_space=pltpu.HBM)
    return pl.pallas_call(
        kernel,
        out_shape=outs,
        in_specs=[raw if i in anywhere else spec for i in range(len(args))],
        out_specs=jax.tree.map(lambda _: spec, outs),
        scratch_shapes=scratch,
        compiler_params=pltpu.CompilerParams(vmem_limit_bytes=16 * 2**20),
        cost_estimate=pl.CostEstimate(flops=flops, bytes_accessed=size, transcendentals=0),
        name=name,
    )(*(pltpu.with_memory_space_constraint(x, pltpu.HBM) if i in anywhere else x for i, x in enumerate(args)))


def per_device(partials, regions, observed, weights, mascons, prior):
    owners, blocks = lax.axis_size("reg"), lax.axis_size("arc")
    arcs, slots = regions.shape
    epochs = observed.shape[1]
    group, width = mascons.shape[0], mascons.shape[2]
    count = arcs * slots
    cap = count // owners
    shape = jax.ShapeDtypeStruct

    def crossing(even, odd):
        return [
            (r * 2 + s, (r ^ (odd if s else even)) * 2 + (1 - s)) for r in range(owners) for s in range(2)
        ]

    names = ("reg", "sat")
    share = group // (blocks * lax.axis_size("sat"))
    whole = (count, epochs, width)
    dma = pltpu.SemaphoreType.DMA
    far_first = list(range(owners - 1, 0, -1))
    pairs = [(k + 1, k) for k in range(owners - 2, 0, -2)]
    hands = [*pairs, (1, 1)]
    asked = {h: lax.ppermute(regions, names, crossing(*h)) for h in hands}
    other = lax.ppermute(partials, "sat", [(0, 1), (1, 0)])
    loads = [regions, observed, weights, partials.reshape(whole)]
    table, ids, residuals, precisions, own_partials = call(
        load_kernel,
        "load",
        [shape((group, width), BF16), *(shape(i.shape, i.dtype) for i in loads)],
        [mascons, *loads],
        group * width,
        group * width * 4,
        [VMEM((group, width), F32), dma((4 + len(loads),))],
        range(1 + len(loads)),
    )
    found, came = {}, {}
    for h in hands:
        [found[h]] = call(
            functools.partial(lookup_kernel, cap),
            "lookup",
            [shape((cap, width), BF16)],
            [asked[h], table],
            2 * count * group * width,
            group * width * 4,
        )
    for h in hands:
        rows = found[h]
        if h in pairs:
            rows, _ = lax.optimization_barrier((rows, asked[1, 1]))
        came[h] = lax.ppermute(rows, names, crossing(*h[::-1]))
    ids, _ = lax.optimization_barrier((ids, found[pairs[0]]))
    own, near, far, named, turned = call(
        functools.partial(plan_kernel, cap, owners, pairs),
        "plan",
        [
            shape((count, width), F32),
            shape((count, (owners - 1) * cap), F32),
            shape((count, owners * cap), F32),
            shape((owners * cap, LANES), F32),
            shape((epochs, 2 * arcs), F32),
        ],
        [ids, residuals, precisions, table],
        count * count * width,
        count * width * 4,
    )
    diff = call(
        differ_kernel,
        "differ",
        shape(whole, F32),
        [own_partials, other.reshape(whole)],
        count * epochs * width,
        count * epochs * width * 8,
    )
    arrived = []
    for h in pairs:
        rows, _ = lax.optimization_barrier((came[h], turned))
        arrived += [came[h], lax.ppermute(rows, "sat", [(0, 1), (1, 0)])]
    arrived.append(came[1, 1])
    sent = call(
        functools.partial(solve_kernel, cap, owners),
        "solve",
        [shape((cap, width + LANES), BF16)] * owners,
        [*arrived, own, near, far, named, turned, diff],
        4 * count * epochs * width,
        count * epochs * width * 4,
    )
    mine = [sent[0]] + [lax.ppermute(sent[k], names, crossing(k, k)) for k in far_first]
    mine = jnp.stack(mine)
    if blocks == 2:
        over = [(a * 2 + s, (1 - a) * 2 + (1 - s)) for a in range(2) for s in range(2)]
        early, late = [mine], [lax.ppermute(mine, ("arc", "sat"), over)]
    else:
        early, late = [], [lax.all_gather(mine, "arc", tiled=True)]
    base = call(
        base_kernel,
        "base",
        shape((share, width), F32),
        [mascons, prior.reshape(1, width), *early],
        2 * share * width * count,
        share * width * 8,
        [VMEM((share, 1, width), F32), dma],
        (0,),
    )
    return call(
        functools.partial(place_kernel, group),
        "place",
        shape((share, 1, width), F32),
        [*late, base],
        2 * share * width * blocks * count,
        share * width * 8,
    )


def solution(mesh):
    placed = (
        P(("grp", "arc", "reg"), None, "sat", None, None),
        P(("grp", "arc", "reg"), None),
        P(("grp", "arc", "reg"), None),
        P(("grp", "arc", "reg"), None),
        P(None, ("grp", "reg"), None),
        P(),
    )
    return jax.shard_map(
        per_device,
        mesh=mesh,
        in_specs=placed,
        out_specs=P(("arc", "sat"), ("grp", "reg"), None),
        check_vma=False,
    )
```

```python
import functools

import jax
import jax.numpy as jnp
from jax import lax
from jax.experimental import pallas as pl
from jax.experimental.pallas import tpu as pltpu
from jax.sharding import PartitionSpec as P

F32, BF16, I32 = jnp.float32, jnp.bfloat16, jnp.int32
VMEM = pltpu.VMEM
LANES = 128


def iota(shape, dim):
    return lax.broadcasted_iota(I32, shape, dim)


def transposed_dot(a, b):
    return lax.dot_general(a, b, (((0,), (0,)), ((), ())), preferred_element_type=F32)


def column(refs):
    arcs, slots = refs[0].shape
    rows = [jnp.broadcast_to(ref[a : a + 1, :], (slots, slots)) for ref in refs for a in range(arcs)]
    spread = jnp.concatenate(rows, axis=0)
    mine = iota(spread.shape, 1) == iota(spread.shape, 0) % slots
    return jnp.sum(jnp.where(mine, spread, 0), axis=1, keepdims=True)


def rows_of(local, table):
    onehot = (local == iota((local.shape[0], table.shape[0]), 1)).astype(F32).astype(BF16)
    return jnp.dot(onehot, table[...], preferred_element_type=F32)


def lookup_kernel(cap, *refs):
    n = (len(refs) - 1) // 2
    ids, table, outs = refs[:n], refs[n], refs[n + 1 :]
    group = table.shape[0]
    col = column(ids)
    count = col.shape[0]
    each = count // n
    local = col - lax.axis_index("reg") * group
    owned = (local >= 0) & (local < group)
    dense = rows_of(local, table).astype(BF16)
    row, other = iota((count, count), 0), iota((count, count), 1)
    before = ((other < row) & (other // each == row // each)).astype(F32).astype(BF16)
    members = jnp.broadcast_to(owned.astype(F32), (count, n * cap)).astype(BF16)
    rank = jnp.dot(before, members, preferred_element_type=F32).astype(I32)
    place = rank + (iota(rank.shape, 0) // each) * cap
    pack = (owned & (place == iota(rank.shape, 1))).astype(F32).astype(BF16)
    packed = transposed_dot(pack, dense)
    for k in range(n):
        outs[k][...] = packed[k * cap : (k + 1) * cap].astype(BF16)


def load_kernel(mascons, *refs):
    n = (len(refs) - 3) // 2
    others, table, outs = refs[:n], refs[n], refs[n + 1 : 2 * n + 1]
    held, sems = refs[2 * n + 1 :]
    copies = [pltpu.make_async_copy(mascons.at[:, 0, :], held, sems.at[n])]
    for j, (i, o) in enumerate(zip(others, outs)):
        copies.append(pltpu.make_async_copy(i, o, sems.at[j]))
    for copy in copies:
        copy.start()
    copies[0].wait()
    table[...] = held[...].astype(BF16)
    for copy in copies[1:]:
        copy.wait()


def plan_kernel(cap, owners, pairs, ids, observed, weights, table, *refs):
    own_ref, near_ref, far_ref, names_ref, turned_ref = refs
    me = lax.axis_index("reg")
    sign = 1.0 - 2.0 * lax.axis_index("sat").astype(F32)
    group = table.shape[0]
    col = column([ids])
    count = col.shape[0]
    own_ref[...] = rows_of(col - me * group, table) * sign
    owner = col // group
    member = (owner == iota((count, owners), 1)).astype(F32)
    before = (iota((count, count), 1) < iota((count, count), 0)).astype(F32).astype(BF16)
    ahead = jnp.dot(before, member.astype(BF16), preferred_element_type=F32)
    rank = jnp.sum(member * ahead, axis=1, keepdims=True).astype(I32)
    valid = owner < owners
    step = owner ^ me
    spot = iota(near_ref.shape, 1)
    sat = lax.axis_index("sat")
    turn = jnp.where(step == 1, 2 * len(pairs) * cap, 0)
    for j, (high, low) in enumerate(pairs):
        turn += jnp.where(step == high, (2 * j + sat) * cap, 0)
        turn += jnp.where(step == low, (2 * j + 1 - sat) * cap, 0)
    near = valid & (step > 0) & (spot == turn + rank)
    far = (valid & (iota(far_ref.shape, 1) == step * cap + rank)).astype(F32)
    local = jnp.broadcast_to((col - owner * group - group // 2).astype(F32), (count, names_ref.shape[1]))
    near_ref[...] = near.astype(F32) * sign
    far_ref[...] = far * sign
    names_ref[...] = transposed_dot(far.astype(BF16), local.astype(BF16))
    turned_ref[...] = jnp.concatenate([observed[...], weights[...]], axis=0).T


def differ_kernel(mine, other, diff):
    for i in range(diff.shape[0]):
        diff[i] = mine[i].astype(F32) - other[i].astype(F32)


def solve_kernel(cap, owners, *refs):
    came, outs = refs[: owners - 1], refs[-owners:]
    own_ref, near_ref, far_ref, names_ref, turned, diff = refs[owners - 1 : -owners]
    arcs = turned.shape[1] // 2
    slots = diff.shape[0] // arcs
    came = jnp.concatenate([r[...].astype(F32) for r in came], axis=0).astype(BF16)
    rows = own_ref[...] + jnp.dot(near_ref[...].astype(BF16), came, preferred_element_type=F32)
    parts = []
    for a in range(arcs):
        total = None
        for k in range(slots):
            i = a * slots + k
            term = diff[i] * rows[i : i + 1, :]
            total = term if total is None else total + term
        predicted = jnp.sum(total, axis=1, keepdims=True)
        weighted = turned[:, arcs + a : arcs + a + 1] * (turned[:, a : a + 1] - predicted)
        weighted = weighted.astype(BF16).astype(F32)
        for k in range(slots):
            parts.append(jnp.sum(diff[a * slots + k] * weighted, axis=0, keepdims=True))
    contribution = jnp.concatenate(parts, axis=0).astype(BF16)
    packed = transposed_dot(far_ref[...].astype(BF16), contribution)
    for k in range(owners):
        part = slice(k * cap, (k + 1) * cap)
        outs[k][...] = jnp.concatenate([packed[part], names_ref[part, :]], axis=1).astype(BF16)


def placed_rows(arrived, group, share, width):
    block = lax.axis_index("arc") * lax.axis_size("sat") + lax.axis_index("sat")
    got = jnp.concatenate([r[s].astype(F32) for r in arrived for s in range(r.shape[0])], axis=0)
    local = got[:, width:].astype(I32) + group // 2 - block * share
    local = jnp.concatenate([local] * -(-share // local.shape[1]), axis=1)
    onehot = (local == iota(local.shape, 1)).astype(F32).astype(BF16)
    return transposed_dot(onehot, got[:, :width].astype(BF16))[:share]


def base_kernel(mascons, prior, *refs):
    *arrived, out, held, sem = refs
    share, width = out.shape
    block = lax.axis_index("arc") * lax.axis_size("sat") + lax.axis_index("sat")
    copy = pltpu.make_async_copy(mascons.at[pl.ds(block * share, share)], held, sem)
    copy.start()
    placed = placed_rows(arrived, mascons.shape[0], share, width) if arrived else 0.0
    copy.wait()
    out[...] = placed - prior[...] * held[:, 0, :]


def place_kernel(group, *refs):
    *arrived, base, out = refs
    share, _, width = out.shape
    out[:, 0, :] = base[...] + placed_rows(arrived, group, share, width)


def call(kernel, name, outs, args, flops, size, scratch=(), anywhere=()):
    spec, raw = pl.BlockSpec(memory_space=VMEM), pl.BlockSpec(memory_space=pltpu.HBM)
    return pl.pallas_call(
        kernel,
        out_shape=outs,
        in_specs=[raw if i in anywhere else spec for i in range(len(args))],
        out_specs=jax.tree.map(lambda _: spec, outs),
        scratch_shapes=scratch,
        compiler_params=pltpu.CompilerParams(vmem_limit_bytes=16 * 2**20),
        cost_estimate=pl.CostEstimate(flops=flops, bytes_accessed=size, transcendentals=0),
        name=name,
    )(*(pltpu.with_memory_space_constraint(x, pltpu.HBM) if i in anywhere else x for i, x in enumerate(args)))


def per_device(partials, regions, observed, weights, mascons, prior):
    owners, blocks = lax.axis_size("reg"), lax.axis_size("arc")
    arcs, slots = regions.shape
    epochs = observed.shape[1]
    group, width = mascons.shape[0], mascons.shape[2]
    count = arcs * slots
    cap = count // owners
    shape = jax.ShapeDtypeStruct

    def crossing(even, odd):
        return [
            (r * 2 + s, (r ^ (odd if s else even)) * 2 + (1 - s)) for r in range(owners) for s in range(2)
        ]

    names = ("reg", "sat")
    share = group // (blocks * lax.axis_size("sat"))
    whole = (count, epochs, width)
    dma = pltpu.SemaphoreType.DMA
    far_first = list(range(owners - 1, 0, -1))
    pairs = [(k + 1, k) for k in range(owners - 2, 0, -2)]
    hands = [*pairs, (1, 1)]
    asked = {h: lax.ppermute(regions, names, crossing(*h)) for h in hands}
    other = lax.ppermute(partials, "sat", [(0, 1), (1, 0)])
    loads = [regions, observed, weights, partials.reshape(whole)]
    table, ids, residuals, precisions, own_partials = call(
        load_kernel,
        "load",
        [shape((group, width), BF16), *(shape(i.shape, i.dtype) for i in loads)],
        [mascons, *loads],
        group * width,
        group * width * 4,
        [VMEM((group, width), F32), dma((1 + len(loads),))],
        range(1 + len(loads)),
    )
    found, came = {}, {}
    for h in hands:
        [found[h]] = call(
            functools.partial(lookup_kernel, cap),
            "lookup",
            [shape((cap, width), BF16)],
            [asked[h], table],
            2 * count * group * width,
            group * width * 4,
        )
    for h in hands:
        rows = found[h]
        if h in pairs:
            rows, _ = lax.optimization_barrier((rows, asked[1, 1]))
        came[h] = lax.ppermute(rows, names, crossing(*h[::-1]))
    ids, _ = lax.optimization_barrier((ids, found[pairs[0]]))
    own, near, far, named, turned = call(
        functools.partial(plan_kernel, cap, owners, pairs),
        "plan",
        [
            shape((count, width), F32),
            shape((count, (owners - 1) * cap), F32),
            shape((count, owners * cap), F32),
            shape((owners * cap, LANES), F32),
            shape((epochs, 2 * arcs), F32),
        ],
        [ids, residuals, precisions, table],
        count * count * width,
        count * width * 4,
    )
    diff = call(
        differ_kernel,
        "differ",
        shape(whole, F32),
        [own_partials, other.reshape(whole)],
        count * epochs * width,
        count * epochs * width * 8,
    )
    arrived = []
    for h in pairs:
        rows, _ = lax.optimization_barrier((came[h], turned))
        arrived += [came[h], lax.ppermute(rows, "sat", [(0, 1), (1, 0)])]
    arrived.append(came[1, 1])
    sent = call(
        functools.partial(solve_kernel, cap, owners),
        "solve",
        [shape((cap, width + LANES), BF16)] * owners,
        [*arrived, own, near, far, named, turned, diff],
        4 * count * epochs * width,
        count * epochs * width * 4,
    )
    mine = [sent[0]] + [lax.ppermute(sent[k], names, crossing(k, k)) for k in far_first]
    mine = jnp.stack(mine)
    if blocks == 2:
        over = [(a * 2 + s, (1 - a) * 2 + (1 - s)) for a in range(2) for s in range(2)]
        early, late = [mine], [lax.ppermute(mine, ("arc", "sat"), over)]
    else:
        early, late = [], [lax.all_gather(mine, "arc", tiled=True)]
    base = call(
        base_kernel,
        "base",
        shape((share, width), F32),
        [mascons, prior.reshape(1, width), *early],
        2 * share * width * count,
        share * width * 8,
        [VMEM((share, 1, width), F32), dma],
        (0,),
    )
    return call(
        functools.partial(place_kernel, group),
        "place",
        shape((share, 1, width), F32),
        [*late, base],
        2 * share * width * blocks * count,
        share * width * 8,
    )


def solution(mesh):
    placed = (
        P(("grp", "arc", "reg"), None, "sat", None, None),
        P(("grp", "arc", "reg"), None),
        P(("grp", "arc", "reg"), None),
        P(("grp", "arc", "reg"), None),
        P(None, ("grp", "reg"), None),
        P(),
    )
    return jax.shard_map(
        per_device,
        mesh=mesh,
        in_specs=placed,
        out_specs=P(("arc", "sat"), ("grp", "reg"), None),
        check_vma=False,
    )
```

```python
import functools

import jax
import jax.numpy as jnp
from jax import lax
from jax.experimental import pallas as pl
from jax.experimental.pallas import tpu as pltpu
from jax.sharding import PartitionSpec as P

F32, BF16, I32 = jnp.float32, jnp.bfloat16, jnp.int32
VMEM = pltpu.VMEM
LANES = 128


def iota(shape, dim):
    return lax.broadcasted_iota(I32, shape, dim)


def transposed_dot(a, b):
    return lax.dot_general(a, b, (((0,), (0,)), ((), ())), preferred_element_type=F32)


def column(refs):
    arcs, slots = refs[0].shape
    rows = [jnp.broadcast_to(ref[a : a + 1, :], (slots, slots)) for ref in refs for a in range(arcs)]
    spread = jnp.concatenate(rows, axis=0)
    mine = iota(spread.shape, 1) == iota(spread.shape, 0) % slots
    return jnp.sum(jnp.where(mine, spread, 0), axis=1, keepdims=True)


def rows_of(local, table):
    onehot = (local == iota((local.shape[0], table.shape[0]), 1)).astype(F32).astype(BF16)
    return jnp.dot(onehot, table[...], preferred_element_type=F32)


def lookup_kernel(cap, *refs):
    n = (len(refs) - 1) // 2
    ids, table, outs = refs[:n], refs[n], refs[n + 1 :]
    group = table.shape[0]
    col = column(ids)
    count = col.shape[0]
    each = count // n
    local = col - lax.axis_index("reg") * group
    owned = (local >= 0) & (local < group)
    dense = rows_of(local, table).astype(BF16)
    row, other = iota((count, count), 0), iota((count, count), 1)
    before = ((other < row) & (other // each == row // each)).astype(F32).astype(BF16)
    members = jnp.broadcast_to(owned.astype(F32), (count, n * cap)).astype(BF16)
    rank = jnp.dot(before, members, preferred_element_type=F32).astype(I32)
    place = rank + (iota(rank.shape, 0) // each) * cap
    pack = (owned & (place == iota(rank.shape, 1))).astype(F32).astype(BF16)
    packed = transposed_dot(pack, dense)
    for k in range(n):
        outs[k][...] = packed[k * cap : (k + 1) * cap].astype(BF16)


def load_kernel(mascons, *refs):
    n = (len(refs) - 3) // 2
    others, table, outs = refs[:n], refs[n], refs[n + 1 : 2 * n + 1]
    held, sems = refs[2 * n + 1 :]
    copies = [pltpu.make_async_copy(mascons.at[:, 0, :], held, sems.at[n])]
    for j, (i, o) in enumerate(zip(others, outs)):
        copies.append(pltpu.make_async_copy(i, o, sems.at[j]))
    for copy in copies:
        copy.start()
    copies[0].wait()
    table[...] = held[...].astype(BF16)
    for copy in copies[1:]:
        copy.wait()


def plan_kernel(cap, owners, pairs, ids, observed, weights, table, *refs):
    own_ref, near_ref, far_ref, names_ref, turned_ref = refs
    me = lax.axis_index("reg")
    sign = 1.0 - 2.0 * lax.axis_index("sat").astype(F32)
    group = table.shape[0]
    col = column([ids])
    count = col.shape[0]
    own_ref[...] = rows_of(col - me * group, table) * sign
    owner = col // group
    member = (owner == iota((count, owners), 1)).astype(F32)
    before = (iota((count, count), 1) < iota((count, count), 0)).astype(F32).astype(BF16)
    ahead = jnp.dot(before, member.astype(BF16), preferred_element_type=F32)
    rank = jnp.sum(member * ahead, axis=1, keepdims=True).astype(I32)
    valid = owner < owners
    step = owner ^ me
    spot = iota(near_ref.shape, 1)
    sat = lax.axis_index("sat")
    turn = jnp.where(step == 1, 2 * len(pairs) * cap, 0)
    for j, (high, low) in enumerate(pairs):
        turn += jnp.where(step == high, (2 * j + sat) * cap, 0)
        turn += jnp.where(step == low, (2 * j + 1 - sat) * cap, 0)
    near = valid & (step > 0) & (spot == turn + rank)
    far = (valid & (iota((count, far_ref.shape[0]), 1) == step * cap + rank)).astype(F32)
    local = jnp.broadcast_to((col - owner * group - group // 2).astype(F32), (count, names_ref.shape[1]))
    near_ref[...] = near.astype(F32) * sign
    far_ref[...] = (far * sign).T
    names_ref[...] = transposed_dot(far.astype(BF16), local.astype(BF16))
    turned_ref[...] = jnp.concatenate([observed[...], weights[...]], axis=0).T


def differ_kernel(mine, other, diff):
    for i in range(diff.shape[0]):
        diff[i] = mine[i].astype(F32) - other[i].astype(F32)


def solve_kernel(cap, owners, *refs):
    came, outs = refs[: owners - 1], refs[-owners:]
    own_ref, near_ref, far_ref, names_ref, turned, diff = refs[owners - 1 : -owners]
    arcs = turned.shape[1] // 2
    slots = diff.shape[0] // arcs
    came = jnp.concatenate([r[...].astype(F32) for r in came], axis=0).astype(BF16)
    rows = own_ref[...] + jnp.dot(near_ref[...].astype(BF16), came, preferred_element_type=F32)
    parts = []
    for a in range(arcs):
        total = None
        for k in range(slots):
            i = a * slots + k
            term = diff[i] * rows[i : i + 1, :]
            total = term if total is None else total + term
        predicted = jnp.sum(total, axis=1, keepdims=True)
        weighted = turned[:, arcs + a : arcs + a + 1] * (turned[:, a : a + 1] - predicted)
        weighted = weighted.astype(BF16).astype(F32)
        for k in range(slots):
            parts.append(jnp.sum(diff[a * slots + k] * weighted, axis=0, keepdims=True))
    contribution = jnp.concatenate(parts, axis=0).astype(BF16)
    packed = jnp.dot(far_ref[...].astype(BF16), contribution, preferred_element_type=F32)
    for k in range(owners):
        part = slice(k * cap, (k + 1) * cap)
        outs[k][...] = jnp.concatenate([packed[part], names_ref[part, :]], axis=1).astype(BF16)


def placed_rows(arrived, group, share, width):
    block = lax.axis_index("arc") * lax.axis_size("sat") + lax.axis_index("sat")
    got = jnp.concatenate([r[s].astype(F32) for r in arrived for s in range(r.shape[0])], axis=0)
    local = got[:, width:].astype(I32) + group // 2 - block * share
    local = jnp.concatenate([local] * -(-share // local.shape[1]), axis=1)
    onehot = (local == iota(local.shape, 1)).astype(F32).astype(BF16)
    return transposed_dot(onehot, got[:, :width].astype(BF16))[:share]


def base_kernel(mascons, prior, *refs):
    *arrived, out, held, sem = refs
    share, width = out.shape
    block = lax.axis_index("arc") * lax.axis_size("sat") + lax.axis_index("sat")
    copy = pltpu.make_async_copy(mascons.at[pl.ds(block * share, share)], held, sem)
    copy.start()
    placed = placed_rows(arrived, mascons.shape[0], share, width) if arrived else 0.0
    copy.wait()
    out[...] = placed - prior[...] * held[:, 0, :]


def place_kernel(group, *refs):
    *arrived, base, out = refs
    share, _, width = out.shape
    out[:, 0, :] = base[...] + placed_rows(arrived, group, share, width)


def call(kernel, name, outs, args, flops, size, scratch=(), anywhere=()):
    spec, raw = pl.BlockSpec(memory_space=VMEM), pl.BlockSpec(memory_space=pltpu.HBM)
    return pl.pallas_call(
        kernel,
        out_shape=outs,
        in_specs=[raw if i in anywhere else spec for i in range(len(args))],
        out_specs=jax.tree.map(lambda _: spec, outs),
        scratch_shapes=scratch,
        compiler_params=pltpu.CompilerParams(vmem_limit_bytes=16 * 2**20),
        cost_estimate=pl.CostEstimate(flops=flops, bytes_accessed=size, transcendentals=0),
        name=name,
    )(*(pltpu.with_memory_space_constraint(x, pltpu.HBM) if i in anywhere else x for i, x in enumerate(args)))


def per_device(partials, regions, observed, weights, mascons, prior):
    owners, blocks = lax.axis_size("reg"), lax.axis_size("arc")
    arcs, slots = regions.shape
    epochs = observed.shape[1]
    group, width = mascons.shape[0], mascons.shape[2]
    count = arcs * slots
    cap = count // owners
    shape = jax.ShapeDtypeStruct

    def crossing(even, odd):
        return [
            (r * 2 + s, (r ^ (odd if s else even)) * 2 + (1 - s)) for r in range(owners) for s in range(2)
        ]

    names = ("reg", "sat")
    share = group // (blocks * lax.axis_size("sat"))
    whole = (count, epochs, width)
    dma = pltpu.SemaphoreType.DMA
    far_first = list(range(owners - 1, 0, -1))
    pairs = [(k + 1, k) for k in range(owners - 2, 0, -2)]
    hands = [*pairs, (1, 1)]
    asked = {h: lax.ppermute(regions, names, crossing(*h)) for h in hands}
    other = lax.ppermute(partials, "sat", [(0, 1), (1, 0)])
    loads = [regions, observed, weights, partials.reshape(whole)]
    table, ids, residuals, precisions, own_partials = call(
        load_kernel,
        "load",
        [shape((group, width), BF16), *(shape(i.shape, i.dtype) for i in loads)],
        [mascons, *loads],
        group * width,
        group * width * 4,
        [VMEM((group, width), F32), dma((1 + len(loads),))],
        range(1 + len(loads)),
    )
    found, came = {}, {}
    for h in hands:
        [found[h]] = call(
            functools.partial(lookup_kernel, cap),
            "lookup",
            [shape((cap, width), BF16)],
            [asked[h], table],
            2 * count * group * width,
            group * width * 4,
        )
    for h in hands:
        rows = found[h]
        if h in pairs:
            rows, _ = lax.optimization_barrier((rows, asked[1, 1]))
        came[h] = lax.ppermute(rows, names, crossing(*h[::-1]))
    ids, _ = lax.optimization_barrier((ids, found[pairs[0]]))
    own, near, far, named, turned = call(
        functools.partial(plan_kernel, cap, owners, pairs),
        "plan",
        [
            shape((count, width), F32),
            shape((count, (owners - 1) * cap), F32),
            shape((owners * cap, count), F32),
            shape((owners * cap, LANES), F32),
            shape((epochs, 2 * arcs), F32),
        ],
        [ids, residuals, precisions, table],
        count * count * width,
        count * width * 4,
    )
    diff = call(
        differ_kernel,
        "differ",
        shape(whole, F32),
        [own_partials, other.reshape(whole)],
        count * epochs * width,
        count * epochs * width * 8,
    )
    arrived = []
    for h in pairs:
        rows, _ = lax.optimization_barrier((came[h], turned))
        arrived += [came[h], lax.ppermute(rows, "sat", [(0, 1), (1, 0)])]
    arrived.append(came[1, 1])
    sent = call(
        functools.partial(solve_kernel, cap, owners),
        "solve",
        [shape((cap, width + LANES), BF16)] * owners,
        [*arrived, own, near, far, named, turned, diff],
        4 * count * epochs * width,
        count * epochs * width * 4,
    )
    mine = [sent[0]] + [lax.ppermute(sent[k], names, crossing(k, k)) for k in far_first]
    mine = jnp.stack(mine)
    if blocks == 2:
        over = [(a * 2 + s, (1 - a) * 2 + (1 - s)) for a in range(2) for s in range(2)]
        early, late = [mine], [lax.ppermute(mine, ("arc", "sat"), over)]
    else:
        early, late = [], [lax.all_gather(mine, "arc", tiled=True)]
    base = call(
        base_kernel,
        "base",
        shape((share, width), F32),
        [mascons, prior.reshape(1, width), *early],
        2 * share * width * count,
        share * width * 8,
        [VMEM((share, 1, width), F32), dma],
        (0,),
    )
    return call(
        functools.partial(place_kernel, group),
        "place",
        shape((share, 1, width), F32),
        [*late, base],
        2 * share * width * blocks * count,
        share * width * 8,
    )


def solution(mesh):
    placed = (
        P(("grp", "arc", "reg"), None, "sat", None, None),
        P(("grp", "arc", "reg"), None),
        P(("grp", "arc", "reg"), None),
        P(("grp", "arc", "reg"), None),
        P(None, ("grp", "reg"), None),
        P(),
    )
    return jax.shard_map(
        per_device,
        mesh=mesh,
        in_specs=placed,
        out_specs=P(("arc", "sat"), ("grp", "reg"), None),
        check_vma=False,
    )
```

```python
import functools

import jax
import jax.numpy as jnp
from jax import lax
from jax.experimental import pallas as pl
from jax.experimental.pallas import tpu as pltpu
from jax.sharding import PartitionSpec as P

F32, BF16, I32 = jnp.float32, jnp.bfloat16, jnp.int32
VMEM = pltpu.VMEM
LANES = 128


def iota(shape, dim):
    return lax.broadcasted_iota(I32, shape, dim)


def transposed_dot(a, b):
    return lax.dot_general(a, b, (((0,), (0,)), ((), ())), preferred_element_type=F32)


def column(refs):
    arcs, slots = refs[0].shape
    rows = [jnp.broadcast_to(ref[a : a + 1, :], (slots, slots)) for ref in refs for a in range(arcs)]
    spread = jnp.concatenate(rows, axis=0)
    mine = iota(spread.shape, 1) == iota(spread.shape, 0) % slots
    return jnp.sum(jnp.where(mine, spread, 0), axis=1, keepdims=True)


def rows_of(local, table):
    onehot = (local == iota((local.shape[0], table.shape[0]), 1)).astype(F32).astype(BF16)
    return jnp.dot(onehot, table[...], preferred_element_type=F32)


def lookup_kernel(cap, *refs):
    n = (len(refs) - 1) // 2
    ids, table, outs = refs[:n], refs[n], refs[n + 1 :]
    group = table.shape[0]
    col = column(ids)
    count = col.shape[0]
    each = count // n
    local = col - lax.axis_index("reg") * group
    owned = (local >= 0) & (local < group)
    dense = rows_of(local, table).astype(BF16)
    row, other = iota((count, count), 0), iota((count, count), 1)
    before = ((other < row) & (other // each == row // each)).astype(F32).astype(BF16)
    members = jnp.broadcast_to(owned.astype(F32), (count, n * cap)).astype(BF16)
    rank = jnp.dot(before, members, preferred_element_type=F32).astype(I32)
    place = rank + (iota(rank.shape, 0) // each) * cap
    pack = (owned & (place == iota(rank.shape, 1))).astype(F32).astype(BF16)
    packed = transposed_dot(pack, dense)
    for k in range(n):
        outs[k][...] = packed[k * cap : (k + 1) * cap].astype(BF16)


def load_kernel(mascons, *refs):
    n = (len(refs) - 3) // 2
    others, table, outs = refs[:n], refs[n], refs[n + 1 : 2 * n + 1]
    held, sems = refs[2 * n + 1 :]
    copies = [pltpu.make_async_copy(mascons.at[:, 0, :], held, sems.at[n])]
    for j, (i, o) in enumerate(zip(others, outs)):
        copies.append(pltpu.make_async_copy(i, o, sems.at[j]))
    for copy in copies:
        copy.start()
    copies[0].wait()
    table[...] = held[...].astype(BF16)
    for copy in copies[1:]:
        copy.wait()


def plan_kernel(cap, owners, pairs, ids, observed, weights, table, *refs):
    own_ref, near_ref, far_ref, names_ref, turned_ref = refs
    me = lax.axis_index("reg")
    sign = 1.0 - 2.0 * lax.axis_index("sat").astype(F32)
    group = table.shape[0]
    col = column([ids])
    count = col.shape[0]
    own_ref[...] = rows_of(col - me * group, table) * sign
    owner = col // group
    member = (owner == iota((count, owners), 1)).astype(F32)
    before = (iota((count, count), 1) < iota((count, count), 0)).astype(F32).astype(BF16)
    ahead = jnp.dot(before, member.astype(BF16), preferred_element_type=F32)
    rank = jnp.sum(member * ahead, axis=1, keepdims=True).astype(I32)
    valid = owner < owners
    step = owner ^ me
    spot = iota(near_ref.shape, 1)
    sat = lax.axis_index("sat")
    turn = jnp.where(step == 1, 2 * len(pairs) * cap, 0)
    for j, (high, low) in enumerate(pairs):
        turn += jnp.where(step == high, (2 * j + sat) * cap, 0)
        turn += jnp.where(step == low, (2 * j + 1 - sat) * cap, 0)
    near = valid & (step > 0) & (spot == turn + rank)
    far = (valid & (iota(far_ref.shape, 1) == step * cap + rank)).astype(F32)
    local = jnp.broadcast_to((col - owner * group - group // 2).astype(F32), (count, names_ref.shape[1]))
    near_ref[...] = near.astype(F32) * sign
    far_ref[...] = far * sign
    names_ref[...] = transposed_dot(far.astype(BF16), local.astype(BF16))
    turned_ref[...] = jnp.concatenate([observed[...], weights[...]], axis=0).T


def differ_kernel(mine, other, diff):
    for i in range(diff.shape[0]):
        diff[i] = mine[i].astype(F32) - other[i].astype(F32)


def solve_kernel(cap, owners, *refs):
    came, outs = refs[: owners - 1], refs[-owners:]
    own_ref, near_ref, far_ref, names_ref, turned, diff = refs[owners - 1 : -owners]
    arcs = turned.shape[1] // 2
    slots = diff.shape[0] // arcs
    came = jnp.concatenate([r[...].astype(F32) for r in came], axis=0).astype(BF16)
    rows = own_ref[...] + jnp.dot(near_ref[...].astype(BF16), came, preferred_element_type=F32)
    parts = []
    for a in range(arcs):
        total = None
        for k in range(slots):
            i = a * slots + k
            row, half = rows[i : i + 1, :], rows.shape[1] // 2
            term = diff[i, :, :half] * row[:, :half] + diff[i, :, half:] * row[:, half:]
            total = term if total is None else total + term
        predicted = jnp.sum(total, axis=1, keepdims=True)
        weighted = turned[:, arcs + a : arcs + a + 1] * (turned[:, a : a + 1] - predicted)
        weighted = weighted.astype(BF16).astype(F32)
        for k in range(slots):
            parts.append(jnp.sum(diff[a * slots + k] * weighted, axis=0, keepdims=True))
    contribution = jnp.concatenate(parts, axis=0).astype(BF16)
    packed = transposed_dot(far_ref[...].astype(BF16), contribution)
    for k in range(owners):
        part = slice(k * cap, (k + 1) * cap)
        outs[k][...] = jnp.concatenate([packed[part], names_ref[part, :]], axis=1).astype(BF16)


def placed_rows(arrived, group, share, width):
    block = lax.axis_index("arc") * lax.axis_size("sat") + lax.axis_index("sat")
    got = jnp.concatenate([r[s].astype(F32) for r in arrived for s in range(r.shape[0])], axis=0)
    local = got[:, width:].astype(I32) + group // 2 - block * share
    local = jnp.concatenate([local] * -(-share // local.shape[1]), axis=1)
    onehot = (local == iota(local.shape, 1)).astype(F32).astype(BF16)
    return transposed_dot(onehot, got[:, :width].astype(BF16))[:share]


def base_kernel(mascons, prior, *refs):
    *arrived, out, held, sem = refs
    share, width = out.shape
    block = lax.axis_index("arc") * lax.axis_size("sat") + lax.axis_index("sat")
    copy = pltpu.make_async_copy(mascons.at[pl.ds(block * share, share)], held, sem)
    copy.start()
    placed = placed_rows(arrived, mascons.shape[0], share, width) if arrived else 0.0
    copy.wait()
    out[...] = placed - prior[...] * held[:, 0, :]


def place_kernel(group, *refs):
    *arrived, base, out = refs
    share, _, width = out.shape
    out[:, 0, :] = base[...] + placed_rows(arrived, group, share, width)


def call(kernel, name, outs, args, flops, size, scratch=(), anywhere=()):
    spec, raw = pl.BlockSpec(memory_space=VMEM), pl.BlockSpec(memory_space=pltpu.HBM)
    return pl.pallas_call(
        kernel,
        out_shape=outs,
        in_specs=[raw if i in anywhere else spec for i in range(len(args))],
        out_specs=jax.tree.map(lambda _: spec, outs),
        scratch_shapes=scratch,
        compiler_params=pltpu.CompilerParams(vmem_limit_bytes=16 * 2**20),
        cost_estimate=pl.CostEstimate(flops=flops, bytes_accessed=size, transcendentals=0),
        name=name,
    )(*(pltpu.with_memory_space_constraint(x, pltpu.HBM) if i in anywhere else x for i, x in enumerate(args)))


def per_device(partials, regions, observed, weights, mascons, prior):
    owners, blocks = lax.axis_size("reg"), lax.axis_size("arc")
    arcs, slots = regions.shape
    epochs = observed.shape[1]
    group, width = mascons.shape[0], mascons.shape[2]
    count = arcs * slots
    cap = count // owners
    shape = jax.ShapeDtypeStruct

    def crossing(even, odd):
        return [
            (r * 2 + s, (r ^ (odd if s else even)) * 2 + (1 - s)) for r in range(owners) for s in range(2)
        ]

    names = ("reg", "sat")
    share = group // (blocks * lax.axis_size("sat"))
    whole = (count, epochs, width)
    dma = pltpu.SemaphoreType.DMA
    far_first = list(range(owners - 1, 0, -1))
    pairs = [(k + 1, k) for k in range(owners - 2, 0, -2)]
    hands = [*pairs, (1, 1)]
    asked = {h: lax.ppermute(regions, names, crossing(*h)) for h in hands}
    other = lax.ppermute(partials, "sat", [(0, 1), (1, 0)])
    loads = [regions, observed, weights, partials.reshape(whole)]
    table, ids, residuals, precisions, own_partials = call(
        load_kernel,
        "load",
        [shape((group, width), BF16), *(shape(i.shape, i.dtype) for i in loads)],
        [mascons, *loads],
        group * width,
        group * width * 4,
        [VMEM((group, width), F32), dma((1 + len(loads),))],
        range(1 + len(loads)),
    )
    found, came = {}, {}
    for h in hands:
        [found[h]] = call(
            functools.partial(lookup_kernel, cap),
            "lookup",
            [shape((cap, width), BF16)],
            [asked[h], table],
            2 * count * group * width,
            group * width * 4,
        )
    for h in hands:
        rows = found[h]
        if h in pairs:
            rows, _ = lax.optimization_barrier((rows, asked[1, 1]))
        came[h] = lax.ppermute(rows, names, crossing(*h[::-1]))
    ids, _ = lax.optimization_barrier((ids, found[pairs[0]]))
    own, near, far, named, turned = call(
        functools.partial(plan_kernel, cap, owners, pairs),
        "plan",
        [
            shape((count, width), F32),
            shape((count, (owners - 1) * cap), F32),
            shape((count, owners * cap), F32),
            shape((owners * cap, LANES), F32),
            shape((epochs, 2 * arcs), F32),
        ],
        [ids, residuals, precisions, table],
        count * count * width,
        count * width * 4,
    )
    diff = call(
        differ_kernel,
        "differ",
        shape(whole, F32),
        [own_partials, other.reshape(whole)],
        count * epochs * width,
        count * epochs * width * 8,
    )
    arrived = []
    for h in pairs:
        rows, _ = lax.optimization_barrier((came[h], turned))
        arrived += [came[h], lax.ppermute(rows, "sat", [(0, 1), (1, 0)])]
    arrived.append(came[1, 1])
    sent = call(
        functools.partial(solve_kernel, cap, owners),
        "solve",
        [shape((cap, width + LANES), BF16)] * owners,
        [*arrived, own, near, far, named, turned, diff],
        4 * count * epochs * width,
        count * epochs * width * 4,
    )
    mine = [sent[0]] + [lax.ppermute(sent[k], names, crossing(k, k)) for k in far_first]
    mine = jnp.stack(mine)
    if blocks == 2:
        over = [(a * 2 + s, (1 - a) * 2 + (1 - s)) for a in range(2) for s in range(2)]
        early, late = [mine], [lax.ppermute(mine, ("arc", "sat"), over)]
    else:
        early, late = [], [lax.all_gather(mine, "arc", tiled=True)]
    base = call(
        base_kernel,
        "base",
        shape((share, width), F32),
        [mascons, prior.reshape(1, width), *early],
        2 * share * width * count,
        share * width * 8,
        [VMEM((share, 1, width), F32), dma],
        (0,),
    )
    return call(
        functools.partial(place_kernel, group),
        "place",
        shape((share, 1, width), F32),
        [*late, base],
        2 * share * width * blocks * count,
        share * width * 8,
    )


def solution(mesh):
    placed = (
        P(("grp", "arc", "reg"), None, "sat", None, None),
        P(("grp", "arc", "reg"), None),
        P(("grp", "arc", "reg"), None),
        P(("grp", "arc", "reg"), None),
        P(None, ("grp", "reg"), None),
        P(),
    )
    return jax.shard_map(
        per_device,
        mesh=mesh,
        in_specs=placed,
        out_specs=P(("arc", "sat"), ("grp", "reg"), None),
        check_vma=False,
    )
```
